128 devices in a mesh: sx: 32 (over z, x, core), sy: 4 (over y).
Axes of the slice: x: 4, y: 4, z: 4, core: 2. Of those that a mesh axis runs over, the one named last changes fastest.
Arguments:
- rhs: float32 [512, 128, 512], P('sx', 'sy'), may hold values from -3 to 3.5
- perm_h: float32 [512, 128, 512], P('sx', 'sy'), may hold values from 0.05 to 20
- perm_v: float32 [512, 128, 512], P('sx', 'sy'), may hold values from 0.01 to 5
- prolong: float32 [2, 512, 128, 512], P(None, 'sx', 'sy'), may hold values from 0.2 to 1
- blk_slot: int32 [2, 512, 512], P(None, 'sx', 'sy'), may hold values from 0 to 2303, as said below
- recv_slot: int32 [2304, 128], P(None, ('sx', 'sy')), may hold values from 0 to 1024, as said below
- coarse_cols: int32 [8, 131072], P(None, ('sx', 'sy')), may hold values from 0 to 9215, as said below
- coarse_off: float32 [8, 131072], P(None, ('sx', 'sy')), may hold values from -0.11 to 0.04
- coarse_diag: float32 [1, 131072], P(None, ('sx', 'sy')), may hold values from 4 to 40
Outputs:
- pressure: float32 [512, 128, 512], P('sx', 'sy')
The draws below stay inside these ranges and needn't reach their ends.
Inputs may be any that keep to these rules, and one draw needn't show every extreme that they name: `blk_slot`: each value names a non-empty entry of its source device's lists, only lists to owners that exist, and every non-empty entry is named by some block. `recv_slot`: the non-empty entries of one list come first and name distinct aggregates; 1024 marks an empty entry, and lists from sources outside the mesh are empty. A device's list to itself is full. `coarse_cols`: offsets name owners that exist.
All inputs are finite; a program needn't handle non-finite values.
Results may differ from the reference program's by a relative error of at most 0.0003.
Values sent between devices are 32-bit elements; how exact they have to be, the bound alone decides.
A program may use at most 192 MiB of HBM per device.

```python
import math
import jax
import jax.numpy as jnp

CX = 16
CY = 32
ZB = 4
KP = 2
AGG_DEV = 1024
CAP = 256
NNZ = 8
SWEEPS = 2
CYCLES = 2
CJ = 4
NX = 512
NY = 128
NZ = 512
NAGG = 131072
N_SX = 32
N_SY = 4
DEVICES = 128


def layout_tables(key):
    base = jax.random.fold_in(key, 17)
    keys = jax.random.split(base, 6)
    grid_x = jnp.arange(N_SX, dtype=jnp.int32)[:, None, None]
    grid_y = jnp.arange(N_SY, dtype=jnp.int32)[None, :, None]
    offset = jnp.arange(9, dtype=jnp.int32)[None, None, :]
    target_x = grid_x + offset // 3 - 1
    target_y = grid_y + offset % 3 - 1
    inside = (target_x >= 0) & (target_x < N_SX) & (target_y >= 0) & (target_y < N_SY)
    popular = jax.random.randint(keys[0], (N_SX, N_SY), 0, 4) == 0
    popular_target = popular[jnp.clip(target_x, 0, N_SX - 1), jnp.clip(target_y, 0, N_SY - 1)]
    cold_counts = jax.random.randint(keys[1], (N_SX, N_SY, 9), 1, CAP // 2 + 1)
    hot_counts = jax.random.randint(keys[2], (N_SX, N_SY, 9), CAP // 2 + 1, CAP + 1)
    counts = jnp.where(popular_target, hot_counts, cold_counts)
    counts = jnp.where(offset == 4, CAP, counts)
    counts = jnp.where(inside, counts, 0)
    start = jax.random.randint(keys[3], (N_SX, N_SY, 9), 0, AGG_DEV)
    entry = jnp.arange(CAP, dtype=jnp.int32)
    filled = entry[None, None, None, :] < counts[..., None]
    slots = jnp.where(filled, (start[..., None] + entry) % AGG_DEV, AGG_DEV).astype(jnp.int32)
    padded = jnp.pad(slots, ((1, 1), (1, 1), (0, 0), (0, 0)), constant_values=AGG_DEV)
    pieces = []
    for source_off in range(9):
        step_x = source_off // 3 - 1
        step_y = source_off % 3 - 1
        pieces.append(padded[1 + step_x:1 + step_x + N_SX, 1 + step_y:1 + step_y + N_SY, 8 - source_off, :])
    recv = jnp.stack(pieces, axis=0)
    recv = recv.transpose(0, 3, 1, 2).reshape(9 * CAP, DEVICES).astype(jnp.int32)
    valid = filled.reshape(DEVICES, 9 * CAP)
    order = jnp.argsort(1 - valid.astype(jnp.int32), axis=1, stable=True).astype(jnp.int32)
    number = jnp.sum(counts.reshape(DEVICES, 9), axis=1)
    refs = KP * CX * CY * ZB
    position = jnp.arange(refs, dtype=jnp.int32)[None, :]
    extra = jax.random.randint(keys[4], (DEVICES, refs), 0, 1048576) % number[:, None]
    pick = jnp.where(position < number[:, None], position, extra)
    flat = jnp.take_along_axis(order, pick, axis=1)
    shuffle_keys = jax.random.split(keys[5], DEVICES)
    flat = jax.vmap(lambda one_key, row: jax.random.permutation(one_key, row))(shuffle_keys, flat)
    blocks = flat.reshape(N_SX, N_SY, KP, CX, CY * ZB).transpose(2, 0, 3, 1, 4)
    blocks = blocks.reshape(KP, NX, NY * ZB).astype(jnp.int32)
    return (blocks, recv)


def draw_blk_slot(key, part):
    return layout_tables(key)[0]


def draw_recv_slot(key, part):
    return layout_tables(key)[1]


def draw_coarse_cols(key, part):
    base = jax.random.fold_in(key, 29)
    first, second = jax.random.split(base)
    offset = jax.random.randint(first, (NNZ, NAGG), 0, 9)
    member = jax.random.randint(second, (NNZ, NAGG), 0, AGG_DEV)
    owner = jnp.arange(NAGG, dtype=jnp.int32)[None, :] // AGG_DEV
    target_x = owner // N_SY + offset // 3 - 1
    target_y = owner % N_SY + offset % 3 - 1
    inside = (target_x >= 0) & (target_x < N_SX) & (target_y >= 0) & (target_y < N_SY)
    offset = jnp.where(inside, offset, 4)
    return (offset * AGG_DEV + member).astype(jnp.int32)


def draw_rhs(key, part):
    return jnp.clip(jax.random.normal(key, (NX, NY, NZ), jnp.float32), -3.0, 3.0)


def levels(key, shape, shards, low, top_value):
    loudness, own = 1.0, jax.random.fold_in(key, 6)
    for axis_at, blocks in shards:
        heights = jnp.exp(jax.random.uniform(jax.random.fold_in(own, axis_at), (blocks,), jnp.float32, low / len(shards), top_value / len(shards)))
        loudness = loudness * jnp.repeat(heights, shape[axis_at] // blocks).reshape([-1 if axis == axis_at else 1 for axis in range(len(shape))])
    return loudness


def setup_inputs(seed: int = 0) -> dict:
    key_list = jax.random.split(jax.random.key(seed), 10)
    return {
        "rhs": draw_rhs(jax.random.fold_in(key_list[9], 71), 0),
        "perm_h": jnp.clip(jnp.exp(math.log(20.0) - 5.9914645 * jax.random.uniform(key_list[1], (NX, NY, NZ), jnp.float32) ** levels(key_list[1], (NX, NY, NZ), ((0, 32), (1, 4)), -0.2, 0.2)), 0.05, 20.0),
        "perm_v": jnp.clip(jnp.exp(math.log(5.0) - 6.214608 * jax.random.uniform(key_list[2], (NX, NY, NZ), jnp.float32) ** levels(key_list[2], (NX, NY, NZ), ((0, 32), (1, 4)), -0.2, 0.2)), 0.01, 5.0),
        "prolong": jnp.clip(0.2 + 0.8 * jax.random.uniform(key_list[3], (KP, NX, NY, NZ), jnp.float32) ** levels(key_list[3], (KP, NX, NY, NZ), ((1, 32), (2, 4)), -0.2, 0.2), 0.2, 1.0),
        "blk_slot": draw_blk_slot(jax.random.fold_in(key_list[9], 71), 0),
        "recv_slot": draw_recv_slot(jax.random.fold_in(key_list[9], 71), 0),
        "coarse_cols": draw_coarse_cols(jax.random.fold_in(key_list[9], 71), 0),
        "coarse_off": jnp.clip(-0.11 + 0.15 * jax.random.uniform(key_list[7], (NNZ, NAGG), jnp.float32) ** levels(key_list[7], (NNZ, NAGG), ((1, 128),), -0.2, 0.2), -0.11, 0.04),
        "coarse_diag": jnp.clip(jnp.exp(math.log(40.0) - 2.3025851 * jax.random.uniform(key_list[8], (1, NAGG), jnp.float32) ** levels(key_list[8], (1, NAGG), ((1, 128),), -0.2, 0.2)), 4.0, 40.0),
    }


storage_coef = 0.01
cheb_low = 0.25
cheb_high = 2.0
omega = 0.8


def harmonic(left, right):
    return 2.0 * left * right / (left + right)


def couplings(perm_h, perm_v):
    padded = jnp.pad(perm_h, ((1, 1), (1, 1), (0, 0)))
    t_east = harmonic(perm_h, padded[2:, 1:-1])
    t_west = harmonic(perm_h, padded[:-2, 1:-1])
    t_north = harmonic(perm_h, padded[1:-1, 2:])
    t_south = harmonic(perm_h, padded[1:-1, :-2])
    vertical = jnp.pad(perm_v, ((0, 0), (0, 0), (1, 1)))
    t_up = harmonic(perm_v, vertical[:, :, 2:])
    t_down = harmonic(perm_v, vertical[:, :, :-2])
    diag = storage_coef + t_east + t_west + t_north + t_south + t_up + t_down
    return (t_east, t_west, t_north, t_south, t_up, t_down), diag


def operate(field, trans, diag):
    t_east, t_west, t_north, t_south, t_up, t_down = trans
    rimmed = jnp.pad(field, ((1, 1), (1, 1), (0, 0)))
    vertical = jnp.pad(field, ((0, 0), (0, 0), (1, 1)))
    out = diag * field - t_east * rimmed[2:, 1:-1] - t_west * rimmed[:-2, 1:-1]
    out = out - t_north * rimmed[1:-1, 2:] - t_south * rimmed[1:-1, :-2]
    return out - t_up * vertical[:, :, 2:] - t_down * vertical[:, :, :-2]


def smooth(pressure, rhs, apply_op, diag):
    theta = 0.5 * (cheb_high + cheb_low)
    delta = 0.5 * (cheb_high - cheb_low)
    sigma = theta / delta
    rho = 1.0 / sigma
    scaled = (rhs - apply_op(pressure)) / diag
    update = scaled / theta
    for sweep in range(SWEEPS):
        pressure = pressure + update
        if sweep < SWEEPS - 1:
            scaled = (rhs - apply_op(pressure)) / diag
            rho_next = 1.0 / (2.0 * sigma - rho)
            update = rho_next * rho * update + (2.0 * rho_next / delta) * scaled
            rho = rho_next
    return pressure


def jacobi(coarse_rhs, diag_c, off, cols):
    ratio = coarse_rhs / diag_c
    iterate = omega * ratio
    for step in range(CJ):
        coupled = jnp.sum(off * iterate[cols], axis=0)
        iterate = iterate + omega * (ratio - iterate - coupled)
    return iterate


def reference(rhs, perm_h, perm_v, prolong, blk_slot, recv_slot, coarse_cols, coarse_off, coarse_diag):
    trans, diag = couplings(perm_h, perm_v)

    def apply_op(field):
        return operate(field, trans, diag)

    src_x = jnp.arange(NX, dtype=jnp.int32)[None, :, None] // CX
    src_y = jnp.arange(NY * ZB, dtype=jnp.int32)[None, None, :] // (CY * ZB)
    offset = blk_slot // CAP
    entry = blk_slot % CAP
    owner = ((src_x + offset // 3 - 1) * N_SY + src_y + offset % 3 - 1).astype(jnp.int32)
    slot = recv_slot[((8 - offset) * CAP + entry).astype(jnp.int32), owner]
    global_id = (owner * AGG_DEV + slot).astype(jnp.int32)

    rows = jnp.arange(NAGG, dtype=jnp.int32)[None, :] // AGG_DEV
    row_x = rows // N_SY
    row_y = rows % N_SY
    col_off = coarse_cols // AGG_DEV
    col_owner = (row_x + col_off // 3 - 1) * N_SY + row_y + col_off % 3 - 1
    global_cols = (col_owner * AGG_DEV + coarse_cols % AGG_DEV).astype(jnp.int32)

    shaped = prolong.reshape(KP, NX, NY * ZB, 128)
    pressure = jnp.zeros_like(rhs)
    for cycle in range(CYCLES):
        pressure = smooth(pressure, rhs, apply_op, diag)
        resid = rhs - apply_op(pressure)
        partial_value = jnp.sum(shaped * resid.reshape(1, NX, NY * ZB, 128), axis=-1)
        coarse_rhs = jax.ops.segment_sum(partial_value.reshape(-1), global_id.reshape(-1), num_segments=NAGG)
        solved = jacobi(coarse_rhs, coarse_diag[0], coarse_off, global_cols)
        values = solved[global_id]
        correction = jnp.sum(shaped * values[..., None], axis=0).reshape(NX, NY, NZ)
        pressure = pressure + correction
        pressure = smooth(pressure, rhs, apply_op, diag)
    return pressure
```

```python
import functools

import jax
import jax.numpy as jnp
from jax import lax
from jax.experimental import pallas as pl
from jax.experimental.pallas import tpu as pltpu
from jax.sharding import PartitionSpec as P

CYCLES = 2
CJ = 4

storage_coef = 0.01
cheb_low = 0.25
cheb_high = 2.0
omega = 0.8

THETA = 0.5 * (cheb_high + cheb_low)
DELTA = 0.5 * (cheb_high - cheb_low)
SIGMA = THETA / DELTA
RHO0 = 1.0 / SIGMA
RHO1 = 1.0 / (2.0 * SIGMA - RHO0)
ALPHA = RHO1 * RHO0
BETA = 2.0 * RHO1 / DELTA

W = 5
T = 8
NX, NY, NZ = 16, 32, 512
TILES = (NY + 2 * T) // 8
MESH = pl.DeviceIdType.MESH
AROUND = (0, 1, 2, 3, 5, 6, 7, 8)
f32 = jnp.float32


def neighbour(o):
    x = lax.axis_index("sx") + (o // 3 - 1)
    y = lax.axis_index("sy") + (o % 3 - 1)
    there = (x >= 0) & (x < lax.axis_size("sx")) & (y >= 0) & (y < lax.axis_size("sy"))
    return x, y, there


def inverse(value):
    guess = pl.reciprocal(value, approx=True)
    return guess * (2.0 - value * guess)


def harmonic(left, right):
    total = left + right
    return 2.0 * left * right * inverse(jnp.where(total == 0.0, 1.0, total))


def kernel(
    rhs_h, ph_h, pv_h, pr_h, slot_r, recv_r, cols_r, off_r, diag_r, out_h,
    RHS, PH, PV, TE, TN, TU, INV, P0, P1, PR, ZH, ZL, HOT, SLOT, LT, VT, RIDX, INVL,
    OUT, ARR, TAB, REP, LIST, DIA, RAT, Y,
    in_sem, ssem, rsem, csend, crecv,
):
    sub = lax.broadcasted_iota(jnp.int32, (8, 128), 0)
    lane = lax.broadcasted_iota(jnp.int32, (8, 128), 1)
    lane512 = lax.broadcasted_iota(jnp.int32, (8, NZ), 1)

    def rows(j):
        return slice(8 * j, 8 * j + 8)

    center = (slice(W, W + NX), slice(T, T + NY), slice(None))
    loads = [
        pltpu.make_async_copy(src, dst, in_sem.at[n])
        for n, (src, dst) in enumerate(
            [(ph_h, PH.at[center]), (pv_h, PV.at[center]), (rhs_h, RHS.at[center]), (pr_h, PR)]
        )
    ]
    for load in loads:
        load.start()

    bar = pltpu.get_barrier_semaphore()
    for o in AROUND:
        x, y, there = neighbour(o)

        @pl.when(there)
        def _():
            pl.semaphore_signal(bar, inc=1, device_id=(x, y), device_id_type=MESH)

    for array in (PH, PV, RHS, P0):
        for o, strip in ((1, (slice(0, W),)), (7, (slice(W + NX, 2 * W + NX),)),
                         (3, (slice(None), slice(0, T))), (5, (slice(None), slice(T + NY, 2 * T + NY)))):
            _, _, there = neighbour(o)

            @pl.when(jnp.logical_not(there))
            def _():
                view = array.at[strip]
                count = view.shape[0]

                def clear(i, carry):
                    view[i] = jnp.zeros(view.shape[1:], f32)
                    return carry

                lax.fori_loop(0, count, clear, 0)

    peers = sum(neighbour(o)[2].astype(jnp.int32) for o in AROUND)
    pl.semaphore_wait(bar, peers)

    def strip_copies(n, dst, src, base_x, base_y):
        out = []
        for o in AROUND:
            dx, dy = o // 3 - 1, o % 3 - 1
            sx = {-1: (0, W), 0: (0, NX), 1: (NX - W, W)}[dx]
            tx = {-1: W + NX, 0: W, 1: 0}[dx]
            sy = {-1: (0, T), 0: (0, NY), 1: (NY - T, T)}[dy]
            ty = {-1: T + NY, 0: T, 1: 0}[dy]
            x, y, there = neighbour(o)
            copy = pltpu.make_async_remote_copy(
                src.at[pl.ds(base_x + sx[0], sx[1]), pl.ds(base_y + sy[0], sy[1]), :],
                dst.at[pl.ds(tx, sx[1]), pl.ds(ty, sy[1]), :],
                ssem.at[n, o], rsem.at[n, 8 - o], device_id=(x, y), device_id_type=MESH,
            )
            rx = {-1: 0, 0: W, 1: W + NX}[dx]
            ry = {-1: 0, 0: T, 1: T + NY}[dy]
            here = dst.at[pl.ds(rx, sx[1]), pl.ds(ry, sy[1]), :]
            arrive = pltpu.make_async_remote_copy(
                here, here, ssem.at[n, o], rsem.at[n, o], device_id=(x, y), device_id_type=MESH,
            )
            out.append((there, copy, arrive))
        return out

    def go(copies):
        for there, copy, _ in copies:
            @pl.when(there)
            def _():
                copy.start()

    def land(copies):
        for there, copy, arrive in copies:
            @pl.when(there)
            def _():
                arrive.wait_recv()
                copy.wait_send()

    first = [strip_copies(n, dst, src, 0, 0) for n, (dst, src) in enumerate([(PH, ph_h), (PV, pv_h), (RHS, rhs_h)])]
    for copies in first:
        go(copies)

    for k in range(2):
        for x8 in range(2):
            raw = slot_r[k, 8 * x8:8 * x8 + 8, :]
            order = (((lane >> 5) << 3) + (lane & 7)) * 4 + ((lane >> 3) & 3)
            SLOT[pl.ds(16 * k + 8 * x8, 8), :] = jnp.take_along_axis(
                raw, order, axis=1, mode="promise_in_bounds"
            )
    LT[...] = jnp.zeros_like(LT)
    LT[0:32, :] = SLOT[...] & 127
    LT[...] = LT[...].T
    row32 = lax.broadcasted_iota(jnp.int32, (32, 128), 0)
    for kx in range(32):
        line = jnp.broadcast_to(SLOT[kx:kx + 1, :] >> 7, (32, 128))
        HOT[:, kx * 128:(kx + 1) * 128] = (line == row32).astype(f32).astype(jnp.bfloat16)
    RIDX[...] = jnp.full_like(RIDX, 1024)
    for r in range(18):
        RIDX[r:r + 1, :] = recv_r[0:1, r * 128:(r + 1) * 128]
    low = lax.broadcasted_iota(jnp.int32, (128, 128), 0)
    cnum = lax.broadcasted_iota(jnp.int32, (8, 128), 1).astype(f32) + 1.0
    for o in range(9):
        total = jnp.zeros((8, 128), f32)
        for h in range(2):
            ids = RIDX[2 * o + h:2 * o + h + 1, :]
            a = jnp.where(jnp.broadcast_to(ids >> 7, (8, 128)) == sub, cnum + 128.0 * h, 0.0)
            b = (jnp.broadcast_to(ids & 127, (128, 128)) == low).astype(f32)
            total = total + lax.dot_general(
                a.astype(jnp.bfloat16), b.astype(jnp.bfloat16), (((1,), (1,)), ((), ())),
                preferred_element_type=f32,
            )
        INVL[o] = (total + 0.5).astype(jnp.int32) - 1
    for m in range(8):
        DIA[m:m + 1, :] = diag_r[0:1, m * 128:(m + 1) * 128]
    DIA[...] = 1.0 / DIA[...]

    for load in loads:
        load.wait()
    for copies in first:
        land(copies)

    def edge_x(i, carry):
        for j in range(TILES):
            TE[i, rows(j), :] = harmonic(PH[i, rows(j), :], PH[i + 1, rows(j), :])
        return carry

    lax.fori_loop(0, 2 * W + NX - 1, edge_x, 0)

    sub512 = lax.broadcasted_iota(jnp.int32, (8, NZ), 0)

    def edge_yz(i, carry):
        before = None
        for j in range(TILES):
            ctr = PH[i, rows(j), :]
            if j < TILES - 1:
                up = PH[i, 8 * j + 1:8 * j + 9, :]
            else:
                up = pltpu.roll(ctr, 7, 0)
            tn = harmonic(ctr, up)
            TN[i, rows(j), :] = tn
            pv = PV[i, rows(j), :]
            tu = jnp.where(lane512 == NZ - 1, 0.0, harmonic(pv, pltpu.roll(pv, NZ - 1, 1)))
            TU[i, rows(j), :] = tu
            rolled = pltpu.roll(tn, 1, 0)
            down = rolled if before is None else jnp.where(sub512 == 0, before, rolled)
            before = rolled
            total = storage_coef + TE[i, rows(j), :] + TE[i - 1, rows(j), :] + tn + down + tu + pltpu.roll(tu, 1, 1)
            INV[i, rows(j), :] = inverse(total)
        return carry

    lax.fori_loop(1, 2 * W + NX - 1, edge_yz, 0)

    def residual(field, i, j):
        ctr = field[i, rows(j), :]
        acc = RHS[i, rows(j), :] - storage_coef * ctr
        acc = acc + TE[i, rows(j), :] * (field[i + 1, rows(j), :] - ctr)
        acc = acc + TE[i - 1, rows(j), :] * (field[i - 1, rows(j), :] - ctr)
        fz = TU[i, rows(j), :] * (pltpu.roll(ctr, NZ - 1, 1) - ctr)
        acc = acc + fz - pltpu.roll(fz, 1, 1)
        if j < TILES - 1:
            up = field[i, 8 * j + 1:8 * j + 9, :]
        else:
            up = pltpu.roll(ctr, 7, 0)
        fn = TN[i, rows(j), :] * (up - ctr)
        if j > 0:
            fs = TN[i, 8 * j - 1:8 * j + 7, :] * (ctr - field[i, 8 * j - 1:8 * j + 7, :])
        else:
            fs = pltpu.roll(fn, 1, 0)
        return ctr, acc + fn - fs

    def sweep(extent, update):
        tiles = range(TILES) if extent > 0 else range(1, TILES - 1)

        def body(i, carry):
            for j in tiles:
                update(i, j)
            return carry

        lax.fori_loop(W - extent, W + NX + extent, body, 0)

    def start_from_zero(i, j):
        P1[i, rows(j), :] = (1.0 / THETA) * INV[i, rows(j), :] * RHS[i, rows(j), :]

    def sweep_a(i, j):
        ctr, res = residual(P0, i, j)
        P1[i, rows(j), :] = ctr + (1.0 / THETA) * INV[i, rows(j), :] * res

    def sweep_b_first(i, j):
        ctr, res = residual(P1, i, j)
        P0[i, rows(j), :] = (1.0 + ALPHA) * ctr + BETA * INV[i, rows(j), :] * res

    def sweep_b(i, j):
        ctr, res = residual(P1, i, j)
        P0[i, rows(j), :] = (1.0 + ALPHA) * ctr - ALPHA * P0[i, rows(j), :] + BETA * INV[i, rows(j), :] * res

    def restrict(i, carry):
        x = i - W
        for j in range(1, TILES - 1):
            _, res = residual(P0, i, j)
            t = j - 1
            for k in range(2):
                scaled = PR[k, x, 8 * t:8 * t + 8, :] * res
                which = jnp.full((8, 128), 16 * k, jnp.int32) + x
                pieces = []
                for zb in range(4):
                    part = jnp.sum(scaled[:, 128 * zb:128 * zb + 128], axis=1, keepdims=True)
                    b0 = (t * 4 + zb) * 8
                    at = jnp.take_along_axis(LT[b0:b0 + 8, :], which, axis=1, mode="promise_in_bounds")
                    pieces.append(jnp.where(at == lane, jnp.broadcast_to(part, (8, 128)), 0.0))
                for h in range(2):
                    both = jnp.concatenate(pieces[2 * h:2 * h + 2], axis=0)
                    high = both.astype(jnp.bfloat16)
                    at = pl.multiple_of((16 * k + x) * 128, 128) + (t * 4 + 2 * h) * 8
                    at = pl.multiple_of(at, 16)
                    ZH[pl.ds(at, 16), :] = high
                    ZL[pl.ds(at, 16), :] = (both - high.astype(f32)).astype(jnp.bfloat16)
        return carry

    def exchange(parity, src_of, dst):
        out = []
        for o in AROUND:
            x, y, there = neighbour(o)
            copy = pltpu.make_async_remote_copy(
                src_of(o), dst.at[8 - o], csend.at[parity, o], crecv.at[parity, 8 - o],
                device_id=(x, y), device_id_type=MESH,
            )
            arrive = pltpu.make_async_remote_copy(
                dst.at[o], dst.at[o], csend.at[parity, o], crecv.at[parity, o],
                device_id=(x, y), device_id_type=MESH,
            )
            out.append((there, copy, arrive))
        return out

    def coarse():
        listed = jnp.dot(HOT[...], ZH[...], preferred_element_type=f32) + jnp.dot(
            HOT[...], ZL[...], preferred_element_type=f32
        )
        for r in range(18):
            OUT[r // 2, r % 2:r % 2 + 1, :] = listed[r:r + 1, :]
        step = exchange(0, lambda o: OUT.at[o], ARR)
        go(step)
        ARR[4] = OUT[4]
        land(step)
        total = jnp.zeros((8, 128), f32)
        for o in range(9):
            at = INVL[o]
            for h in range(2):
                got = jnp.take_along_axis(
                    jnp.broadcast_to(ARR[o, h:h + 1, :], (8, 128)), at & 127, axis=1, mode="promise_in_bounds"
                )
                total = total + jnp.where((at >> 7) == h, got, 0.0)
        RAT[...] = total * DIA[...]
        Y[...] = omega * RAT[...]
        for s in range(CJ):
            table = TAB.at[s % 2]
            step = exchange((s + 1) % 2, lambda o: Y, table)
            go(step)
            table[4] = Y[...]
            land(step)
            for m in range(8):
                at = cols_r[:, 128 * m:128 * m + 128]
                got = jnp.zeros((8, 128), f32)
                for r in range(72):
                    one = jnp.take_along_axis(
                        jnp.broadcast_to(table[r // 8, r % 8:r % 8 + 1, :], (8, 128)), at & 127,
                        axis=1, mode="promise_in_bounds",
                    )
                    got = jnp.where((at >> 7) == r, one, got)
                coupled = jnp.sum(got * off_r[:, 128 * m:128 * m + 128], axis=0, keepdims=True)
                mine = Y[m:m + 1, :]
                Y[m:m + 1, :] = mine + omega * (RAT[m:m + 1, :] - mine - coupled)
        for r3 in range(3):
            at = RIDX[8 * r3:8 * r3 + 8, :]
            got = jnp.zeros((8, 128), f32)
            for r in range(8):
                one = jnp.take_along_axis(
                    jnp.broadcast_to(Y[r:r + 1, :], (8, 128)), at & 127, axis=1, mode="promise_in_bounds"
                )
                got = jnp.where((at >> 7) == r, one, got)
            for s in range(8):
                r = 8 * r3 + s
                if r < 18:
                    REP[r // 2, r % 2:r % 2 + 1, :] = got[s:s + 1, :]
        step = exchange((CJ + 1) % 2, lambda o: REP.at[o], LIST)
        go(step)
        LIST[4] = REP[4]
        land(step)
        VT[...] = jnp.zeros_like(VT)
        for r4 in range(4):
            at = SLOT[8 * r4:8 * r4 + 8, :]
            got = jnp.zeros((8, 128), f32)
            for r in range(18):
                one = jnp.take_along_axis(
                    jnp.broadcast_to(LIST[r // 2, r % 2:r % 2 + 1, :], (8, 128)), at & 127,
                    axis=1, mode="promise_in_bounds",
                )
                got = jnp.where((at >> 7) == r, one, got)
            VT[8 * r4:8 * r4 + 8, :] = got
        VT[...] = VT[...].T

        def correct(x, carry):
            for t in range(4):
                total = P0[x + W, T + 8 * t:T + 8 * t + 8, :]
                for k in range(2):
                    which = jnp.full((8, 128), 16 * k, jnp.int32) + x
                    spread = []
                    for zb in range(4):
                        b0 = (t * 4 + zb) * 8
                        spread.append(
                            jnp.take_along_axis(VT[b0:b0 + 8, :], which, axis=1, mode="promise_in_bounds")
                        )
                    total = total + PR[k, x, 8 * t:8 * t + 8, :] * jnp.concatenate(spread, axis=1)
                P0[x + W, T + 8 * t:T + 8 * t + 8, :] = total
            return carry

        lax.fori_loop(0, NX, correct, 0)

    for cycle in range(CYCLES):
        if cycle == 0:
            sweep(2, start_from_zero)
            sweep(1, sweep_b_first)
        else:
            sweep(2, sweep_a)
            sweep(1, sweep_b)
        lax.fori_loop(W, W + NX, restrict, 0)
        coarse()
        step = strip_copies(3 + cycle, P0, P0, W, T)
        go(step)
        land(step)
        if cycle == 0:
            sweep(4, sweep_a)
            sweep(3, sweep_b)
        else:
            sweep(1, sweep_a)
            sweep(0, sweep_b)
    back = pltpu.make_async_copy(P0.at[center], out_h, in_sem.at[0])
    back.start()
    back.wait()


def shards(rhs, perm_h, perm_v, prolong, blk_slot, recv_slot, coarse_cols, coarse_off, coarse_diag):
    padded = pltpu.VMEM((2 * W + NX, 2 * T + NY, NZ), f32)
    hbm = pl.BlockSpec(memory_space=pl.ANY)
    vmem = pl.BlockSpec(memory_space=pltpu.VMEM)
    return pl.pallas_call(
        kernel,
        out_shape=jax.ShapeDtypeStruct(rhs.shape, f32),
        in_specs=[hbm] * 4 + [vmem] * 5,
        out_specs=hbm,
        scratch_shapes=[padded] * 9
        + [
            pltpu.VMEM((2, NX, NY, NZ), f32),
            pltpu.VMEM((4096, 128), jnp.bfloat16),
            pltpu.VMEM((4096, 128), jnp.bfloat16),
            pltpu.VMEM((32, 4096), jnp.bfloat16),
            pltpu.VMEM((32, 128), jnp.int32),
            pltpu.VMEM((128, 128), jnp.int32),
            pltpu.VMEM((128, 128), f32),
            pltpu.VMEM((24, 128), jnp.int32),
            pltpu.VMEM((9, 8, 128), jnp.int32),
            pltpu.VMEM((9, 2, 128), f32),
            pltpu.VMEM((9, 2, 128), f32),
            pltpu.VMEM((2, 9, 8, 128), f32),
            pltpu.VMEM((9, 2, 128), f32),
            pltpu.VMEM((9, 2, 128), f32),
            pltpu.VMEM((8, 128), f32),
            pltpu.VMEM((8, 128), f32),
            pltpu.VMEM((8, 128), f32),
            pltpu.SemaphoreType.DMA((4,)),
            pltpu.SemaphoreType.DMA((5, 9)),
            pltpu.SemaphoreType.DMA((5, 9)),
            pltpu.SemaphoreType.DMA((2, 9)),
            pltpu.SemaphoreType.DMA((2, 9)),
        ],
        compiler_params=pltpu.CompilerParams(
            collective_id=0, has_side_effects=True, vmem_limit_bytes=52 << 20
        ),
    )(rhs, perm_h, perm_v, prolong, blk_slot, recv_slot.T, coarse_cols, coarse_off, coarse_diag)


def solution(mesh):
    placed = (
        P("sx", "sy", None),
        P("sx", "sy", None),
        P("sx", "sy", None),
        P(None, "sx", "sy", None),
        P(None, "sx", "sy"),
        P(None, ("sx", "sy")),
        P(None, ("sx", "sy")),
        P(None, ("sx", "sy")),
        P(None, ("sx", "sy")),
    )
    return jax.shard_map(
        shards, mesh=mesh, in_specs=placed, out_specs=P("sx", "sy", None), check_vma=False
    )
```

```python
import functools

import jax
import jax.numpy as jnp
from jax import lax
from jax.experimental import pallas as pl
from jax.experimental.pallas import tpu as pltpu
from jax.sharding import PartitionSpec as P

CYCLES = 2
CJ = 4

storage_coef = 0.01
cheb_low = 0.25
cheb_high = 2.0
omega = 0.8

THETA = 0.5 * (cheb_high + cheb_low)
DELTA = 0.5 * (cheb_high - cheb_low)
SIGMA = THETA / DELTA
RHO0 = 1.0 / SIGMA
RHO1 = 1.0 / (2.0 * SIGMA - RHO0)
ALPHA = RHO1 * RHO0
BETA = 2.0 * RHO1 / DELTA

W = 3
T = 8
NX, NY, NZ = 16, 32, 512
TILES = (NY + 2 * T) // 8
MESH = pl.DeviceIdType.MESH
AROUND = (0, 1, 2, 3, 5, 6, 7, 8)
NEAR = tuple((dx, dy) for dx in range(-2, 3) for dy in range(-2, 3) if (dx, dy) != (0, 0))
f32 = jnp.float32
bf16 = jnp.bfloat16


def neighbour(dx, dy):
    x = lax.axis_index("sx") + dx
    y = lax.axis_index("sy") + dy
    there = (x >= 0) & (x < lax.axis_size("sx")) & (y >= 0) & (y < lax.axis_size("sy"))
    return x, y, there


def inverse(value):
    guess = pl.reciprocal(value, approx=True)
    return guess * (2.0 - value * guess)


def harmonic(left, right):
    total = left + right
    return 2.0 * left * right * inverse(jnp.where(total == 0.0, 1.0, total))


def pick(row, at):
    return jnp.take_along_axis(
        jnp.broadcast_to(row, at.shape), at & 127, axis=1, mode="promise_in_bounds"
    )


def pick_from(table_rows, at):
    high = at >> 7
    got = jnp.zeros(at.shape, f32)
    for r, row in enumerate(table_rows):
        got = jnp.where(high == r, pick(row(), at), got)
    return got


def kernel(
    rhs_h, ph_h, pv_h, pr_h, slot_h, recv_h, cols_h, off_h, diag_h, out_h,
    RHS, PH, PV, TE, TN, TU, INV, P0, P1, P2, PR, PKS, RKS, PKP, RKP, RKC,
    WH, WL, HOT, LHOT, AB, SLOT, LT, VT, RIDX, INVN, DIAN, MSG, ENT,
    OUT, ARR, RATN, TAB, T25, LIST, Y, BASE,
    slot_r, recv_r, cols_r, off_r, diag_r,
    in_sem, fsend, frecv, psend, precv, csend, crecv, wsend, wrecv,
):
    sub = lax.broadcasted_iota(jnp.int32, (8, 128), 0)
    lane = lax.broadcasted_iota(jnp.int32, (8, 128), 1)
    sub512 = lax.broadcasted_iota(jnp.int32, (8, NZ), 0)
    lane512 = lax.broadcasted_iota(jnp.int32, (8, NZ), 1)

    def rows(j):
        return slice(8 * j, 8 * j + 8)

    inner = pl.ds(T, NY)
    center = (pl.ds(W, NX), inner, slice(None))
    loads = [
        pltpu.make_async_copy(src, dst, in_sem.at[n])
        for n, (src, dst) in enumerate(
            [(ph_h, PH.at[center]), (pv_h, PV.at[center]), (rhs_h, RHS.at[center]),
             (slot_h, slot_r), (recv_h, recv_r), (cols_h, cols_r), (off_h, off_r), (diag_h, diag_r),
             (pr_h, PR)]
        )
    ]
    for load in loads:
        load.start()

    bar = pltpu.get_barrier_semaphore()
    for dx, dy in NEAR:
        x, y, there = neighbour(dx, dy)

        @pl.when(there)
        def _():
            pl.semaphore_signal(bar, inc=1, device_id=(x, y), device_id_type=MESH)

    def clear(view):
        def one(i, carry):
            view[i] = jnp.zeros(view.shape[1:], f32)
            return carry

        lax.fori_loop(0, view.shape[0], one, 0)

    for array in (PH, PV, RHS, P0, P2):
        for dx, strip in ((-1, pl.ds(0, W)), (1, pl.ds(W + NX, W))):
            _, _, there = neighbour(dx, 0)

            @pl.when(jnp.logical_not(there))
            def _():
                clear(array.at[strip])

    for i in (0, 2 * W + NX - 1):
        for j in (0, TILES - 1):
            PH[i, rows(j), :] = jnp.zeros((8, NZ), f32)
    for side, dy in ((0, -1), (1, 1)):
        _, _, there = neighbour(0, dy)

        @pl.when(jnp.logical_not(there))
        def _():
            clear(RKS.at[side])
            clear(P0.at[:, pl.ds(0 if side == 0 else T + NY, T), :])
            clear(P2.at[:, pl.ds(0 if side == 0 else T + NY, T), :])

    for dx, strip in ((-1, pl.ds(0, 2)), (1, pl.ds(NX + 2, 2))):
        _, _, there = neighbour(dx, 0)

        @pl.when(jnp.logical_not(there))
        def _():
            clear(RKS.at[0, strip])
            clear(RKS.at[1, strip])

    for load in loads[:3]:
        load.wait()

    def pack_first(x, carry):
        i = x + W
        a, b, c = PH[i, rows(1), :], PV[i, rows(1), :], RHS[i, rows(1), :]
        PKS[0, x] = jnp.where(sub512 < 3, a, jnp.where(sub512 < 5, pltpu.roll(b, 3, 0), pltpu.roll(c, 5, 0)))
        a, b, c = PH[i, rows(4), :], PV[i, rows(4), :], RHS[i, rows(4), :]
        PKS[1, x] = jnp.where(sub512 >= 5, a, jnp.where(sub512 >= 3, pltpu.roll(b, 5, 0), pltpu.roll(c, 3, 0)))
        return carry

    lax.fori_loop(0, NX, pack_first, 0)

    peers = sum(neighbour(dx, dy)[2].astype(jnp.int32) for dx, dy in NEAR)
    pl.semaphore_wait(bar, peers)

    def go(copies):
        for there, copy, _ in copies:
            @pl.when(there)
            def _():
                copy.start()

    def land(copies):
        for there, copy, arrive in copies:
            @pl.when(there)
            def _():
                arrive.wait_recv()
                copy.wait_send()

    def moved(to, src, there_dst, here_dst, send, recv_there, recv_here):
        x, y, there = neighbour(*to)
        copy = pltpu.make_async_remote_copy(
            src, there_dst, send, recv_there, device_id=(x, y), device_id_type=MESH
        )
        arrive = pltpu.make_async_remote_copy(
            here_dst, here_dst, send, recv_here, device_id=(x, y), device_id_type=MESH
        )
        return there, copy, arrive

    def x_strips(field, src, base, width, send, recv):
        out = []
        for dx in (-1, 1):
            if dx < 0:
                take, put, get = base, W + NX, W - width
            else:
                take, put, get = base + NX - width, W - width, W + NX
            pick_y = inner if base else slice(None)
            out.append(moved(
                (dx, 0), src.at[pl.ds(take, width), pick_y, :], field.at[pl.ds(put, width), inner, :],
                field.at[pl.ds(get, width), inner, :],
                send.at[(dx + 1) // 2], recv.at[(1 - dx) // 2], recv.at[(dx + 1) // 2],
            ))
        return out

    first = []
    for dy in (-1, 1):
        side = (dy + 1) // 2
        for dx in (0, -1, 1):
            src = {0: pl.ds(0, NX), -1: pl.ds(0, 2), 1: pl.ds(NX - 2, 2)}[dx]
            put = {0: pl.ds(2, NX), -1: pl.ds(NX + 2, 2), 1: pl.ds(0, 2)}[dx]
            get = {0: pl.ds(2, NX), -1: pl.ds(0, 2), 1: pl.ds(NX + 2, 2)}[dx]
            first.append(moved(
                (dx, dy), PKS.at[side, src], RKS.at[1 - side, put], RKS.at[side, get],
                fsend.at[3, dx + 1 + 3 * side], frecv.at[3, 1 - dx + 3 * (1 - side)],
                frecv.at[3, dx + 1 + 3 * side],
            ))
    for n, (field, src, width) in enumerate(((PH, ph_h, 3), (PV, pv_h, 2), (RHS, rhs_h, 2))):
        first += x_strips(field, src, 0, width, fsend.at[n], frecv.at[n])
    go(first)

    for load in loads[3:]:
        load.wait()
    for k in range(2):
        for x8 in range(2):
            raw = slot_r[k, 8 * x8:8 * x8 + 8, :]
            order = (((lane >> 5) << 3) + (lane & 7)) * 4 + ((lane >> 3) & 3)
            SLOT[pl.ds(16 * k + 8 * x8, 8), :] = jnp.take_along_axis(
                raw, order, axis=1, mode="promise_in_bounds"
            )
    RIDX[...] = jnp.full_like(RIDX, 1024)
    for r in range(18):
        RIDX[r:r + 1, :] = recv_r[0:1, r * 128:(r + 1) * 128]
    low = lax.broadcasted_iota(jnp.int32, (128, 128), 0)
    cnum = lane.astype(f32) + 1.0
    for o in range(9):
        total = jnp.zeros((8, 128), f32)
        for h in range(2):
            ids = RIDX[2 * o + h:2 * o + h + 1, :]
            a = jnp.where(jnp.broadcast_to(ids >> 7, (8, 128)) == sub, cnum + 128.0 * h, 0.0)
            b = (jnp.broadcast_to(ids & 127, (128, 128)) == low).astype(f32)
            total = total + lax.dot_general(
                a.astype(bf16), b.astype(bf16), (((1,), (1,)), ((), ())),
                preferred_element_type=f32,
            )
        INVN[4, o] = (total + 0.5).astype(jnp.int32) - 1
    for m in range(8):
        DIAN[4, m:m + 1, :] = diag_r[0:1, m * 128:(m + 1) * 128]
    DIAN[4] = 1.0 / DIAN[4]
    for o in range(9):
        for h in range(2):
            at = jnp.broadcast_to(RIDX[2 * o + h:2 * o + h + 1, :], (8, 128))
            at = jnp.where(at == 1024, 0, at)
            cols = jnp.zeros((8, 128), f32)
            offs = jnp.zeros((8, 128), f32)
            for m in range(8):
                piece = slice(128 * m, 128 * m + 128)
                hit = (at >> 7) == m
                cols = jnp.where(hit, pick(cols_r[:, piece].astype(f32), at), cols)
                offs = jnp.where(hit, pick(off_r[:, piece], at), offs)
            MSG[o, h, 0:8, :] = cols
            MSG[o, h, 8:16, :] = offs
            MSG[o, h, 16:24, :] = at.astype(f32)
    ENT[4] = MSG[4]

    def around(src, dst, send, recv):
        out = []
        for o in AROUND:
            out.append(moved(
                (o // 3 - 1, o % 3 - 1), src(o), dst.at[8 - o], dst.at[o],
                send.at[o], recv.at[8 - o], recv.at[o],
            ))
        return out

    tables = []
    for o in AROUND:
        to = (o // 3 - 1, o % 3 - 1)
        tables.append(moved(to, INVN.at[4], INVN.at[8 - o], INVN.at[o], wsend.at[0, o], wrecv.at[0, 8 - o], wrecv.at[0, o]))
        tables.append(moved(to, DIAN.at[4], DIAN.at[8 - o], DIAN.at[o], wsend.at[1, o], wrecv.at[1, 8 - o], wrecv.at[1, o]))
    tables += around(lambda o: MSG.at[o], ENT, wsend.at[2], wrecv.at[2])
    go(tables)

    LT[...] = jnp.zeros_like(LT)
    LT[0:32, :] = SLOT[...] & 127
    LT[...] = LT[...].T
    lane_all = lax.broadcasted_iota(jnp.int32, (128, 128), 1)
    row24 = lax.broadcasted_iota(jnp.int32, (24, 128), 0)
    for kx in range(32):
        line = jnp.broadcast_to(SLOT[kx:kx + 1, :] >> 7, (24, 128))
        HOT[:, kx * 128:(kx + 1) * 128] = (line == row24).astype(f32)
        LHOT[kx * 128:(kx + 1) * 128, :] = (
            jnp.broadcast_to(LT[:, kx:kx + 1], (128, 128)) == lane_all
        ).astype(f32).astype(bf16)
    AB[...] = jnp.zeros_like(AB)

    def edge_x(i, tiles):
        for j in tiles:
            TE[i, rows(j), :] = harmonic(PH[i, rows(j), :], PH[i + 1, rows(j), :])

    def edge_yz(i, new, done):
        for j in new:
            ctr = PH[i, rows(j), :]
            if j < TILES - 1:
                up = PH[i, 8 * j + 1:8 * j + 9, :]
            else:
                up = pltpu.roll(ctr, 7, 0)
            TN[i, rows(j), :] = harmonic(ctr, up)
            pv = PV[i, rows(j), :]
            TU[i, rows(j), :] = jnp.where(
                lane512 == NZ - 1, 0.0, harmonic(pv, pltpu.roll(pv, NZ - 1, 1))
            )
        for j in done:
            tn = TN[i, rows(j), :]
            down = TN[i, 8 * j - 1:8 * j + 7, :] if j > 0 else pltpu.roll(tn, 1, 0)
            tu = TU[i, rows(j), :]
            total = storage_coef + TE[i, rows(j), :] + TE[i - 1, rows(j), :] + tn + down + tu + pltpu.roll(tu, 1, 1)
            INV[i, rows(j), :] = inverse(total)

    def loop(lo, hi, fn):
        def body(i, carry):
            fn(i)
            return carry

        lax.fori_loop(lo, hi, body, 0)

    every = tuple(range(TILES))
    loop(W, W + NX - 1, lambda i: edge_x(i, (1, 2, 3, 4)))
    loop(W + 1, W + NX - 1, lambda i: edge_yz(i, (1, 2, 3), (2, 3)))

    land(first)

    def unpack_first(i):
        got = RKS[0, i - 1]
        PH[i, rows(0), :] = jnp.where(sub512 >= 5, got, 0.0)
        PV[i, rows(0), :] = jnp.where(sub512 >= 6, pltpu.roll(got, 3, 0), 0.0)
        RHS[i, rows(0), :] = jnp.where(sub512 >= 6, pltpu.roll(got, 5, 0), 0.0)
        got = RKS[1, i - 1]
        PH[i, rows(5), :] = jnp.where(sub512 < 3, got, 0.0)
        PV[i, rows(5), :] = jnp.where(sub512 < 2, pltpu.roll(got, 5, 0), 0.0)
        RHS[i, rows(5), :] = jnp.where(sub512 < 2, pltpu.roll(got, 3, 0), 0.0)

    loop(1, NX + 5, unpack_first)
    for lo, hi in ((0, W), (W + NX - 1, 2 * W + NX - 1)):
        loop(lo, hi, lambda i: edge_x(i, every))
    loop(W, W + NX - 1, lambda i: edge_x(i, (0, 5)))
    for lo, hi in ((1, W + 1), (W + NX - 1, 2 * W + NX - 1)):
        loop(lo, hi, lambda i: edge_yz(i, every, every))
    loop(W + 1, W + NX - 1, lambda i: edge_yz(i, (0, 4, 5), (0, 1, 4, 5)))

    def residual(field, i, j):
        ctr = field[i, rows(j), :]
        acc = RHS[i, rows(j), :] - storage_coef * ctr
        acc = acc + TE[i, rows(j), :] * (field[i + 1, rows(j), :] - ctr)
        acc = acc + TE[i - 1, rows(j), :] * (field[i - 1, rows(j), :] - ctr)
        fz = TU[i, rows(j), :] * (pltpu.roll(ctr, NZ - 1, 1) - ctr)
        acc = acc + fz - pltpu.roll(fz, 1, 1)
        if j < TILES - 1:
            up = field[i, 8 * j + 1:8 * j + 9, :]
        else:
            up = pltpu.roll(ctr, 7, 0)
        fn = TN[i, rows(j), :] * (up - ctr)
        if j > 0:
            fs = TN[i, 8 * j - 1:8 * j + 7, :] * (ctr - field[i, 8 * j - 1:8 * j + 7, :])
        else:
            fs = pltpu.roll(fn, 1, 0)
        return ctr, acc + fn - fs

    def sweep(extent, update):
        tiles = range(TILES) if extent > 0 else range(1, TILES - 1)

        def body(i):
            for j in tiles:
                update(i, j)

        loop(W - extent, W + NX + extent, body)

    def start_from_zero(i, j):
        P1[i, rows(j), :] = (1.0 / THETA) * INV[i, rows(j), :] * RHS[i, rows(j), :]

    def sweep_a(field, i, j):
        ctr, res = residual(field, i, j)
        P1[i, rows(j), :] = ctr + (1.0 / THETA) * INV[i, rows(j), :] * res

    def sweep_b_first(i, j):
        ctr, res = residual(P1, i, j)
        P0[i, rows(j), :] = (1.0 + ALPHA) * ctr + BETA * INV[i, rows(j), :] * res

    def sweep_b(old, new, i, j):
        ctr, res = residual(P1, i, j)
        new[i, rows(j), :] = (1.0 + ALPHA) * ctr - ALPHA * old[i, rows(j), :] + BETA * INV[i, rows(j), :] * res

    def exchange_pressure(field, width, slot):
        per = 8 // (2 if width == 2 else 4)
        span = 8 // per
        tiles = NX // per

        def pack(g):
            a = b = None
            for m in range(per):
                i = W + g * per + m
                one = field[i, rows(1), :]
                two = field[i, rows(4), :]
                one = one if m == 0 else pltpu.roll(one, m * span, 0)
                two = two if (m + 1) * span == 8 else pltpu.roll(two, (m + 1) * span, 0)
                a = one if a is None else jnp.where(sub512 >= m * span, one, a)
                b = two if b is None else jnp.where(sub512 >= m * span, two, b)
            PKP[0, g] = a
            PKP[1, g] = b

        loop(0, tiles, pack)
        step = x_strips(field, field, W, width, psend.at[slot, 0], precv.at[slot, 0])
        for dy in (-1, 1):
            side = (dy + 1) // 2
            step.append(moved(
                (0, dy), PKP.at[side, pl.ds(0, tiles)], RKP.at[slot, 1 - side, pl.ds(0, tiles)],
                RKP.at[slot, side, pl.ds(0, tiles)],
                psend.at[slot, 1, side], precv.at[slot, 1, 1 - side], precv.at[slot, 1, side],
            ))
            for dx in (-1, 1):
                far = (dx + 1) // 2
                step.append(moved(
                    (dx, dy), PKP.at[side, 0 if dx < 0 else tiles - 1], RKC.at[slot, 1 - side, 1 - far],
                    RKC.at[slot, side, far],
                    psend.at[slot, 2 + side, far], precv.at[slot, 2 + 1 - side, 1 - far], precv.at[slot, 2 + side, far],
                ))
        go(step)
        land(step)

        def place(side, tile, m, i):
            if side == 0:
                turn = (8 - span - m * span) % 8
            else:
                turn = (-m * span) % 8
            tile = pltpu.roll(tile, turn, 0) if turn else tile
            field[i, rows(0 if side == 0 else 5), :] = tile

        for side, dy in ((0, -1), (1, 1)):
            _, _, there = neighbour(0, dy)

            @pl.when(there)
            def _():
                def body(g):
                    tile = RKP[slot, side, g]
                    for m in range(per):
                        place(side, tile, m, W + g * per + m)

                loop(0, tiles, body)

            for far, dx in ((0, -1), (1, 1)):
                _, _, there = neighbour(dx, dy)

                @pl.when(there)
                def _():
                    tile = RKC[slot, side, far]
                    for depth in range(width - 1):
                        if dx < 0:
                            place(side, tile, per - 1 - depth, W - 1 - depth)
                        else:
                            place(side, tile, depth, W + NX + depth)

    def restrict(field, i):
        x = i - W
        for j in range(1, TILES - 1):
            _, res = residual(field, i, j)
            t = j - 1
            for k in range(2):
                scaled = PR[k, x, 8 * t:8 * t + 8, :] * res
                for h in range(2):
                    both = jnp.concatenate(
                        [scaled[:, 256 * h:256 * h + 128], scaled[:, 256 * h + 128:256 * h + 256]], axis=0
                    )
                    high = both.astype(bf16)
                    at = pl.multiple_of((16 * k + x) * 128 + (t * 4 + 2 * h) * 8, 16)
                    WH[pl.ds(at, 16), :] = high
                    WL[pl.ds(at, 16), :] = (both - high.astype(f32)).astype(bf16)

    def wide(src, dst, parity, lists):
        out = []
        for n, (dx, dy) in enumerate(NEAR):
            if lists:
                def rect(ax, ay):
                    x0, x1 = max(-1, ax - 1) + 1, min(1, ax + 1) + 2
                    y0, y1 = max(-1, ay - 1) + 1, min(1, ay + 1) + 2
                    return pl.ds(x0, x1 - x0), pl.ds(y0, y1 - y0)
                give, take = rect(dx, dy), rect(-dx, -dy)
                piece, put, get = src.at[give], dst.at[(2 - dx, 2 - dy) + give], dst.at[(2 + dx, 2 + dy) + take]
            else:
                piece, put, get = src, dst.at[2 - dx, 2 - dy], dst.at[2 + dx, 2 + dy]
            out.append(moved(
                (dx, dy), piece, put, get, wsend.at[3 + parity, n], wrecv.at[3 + parity, 23 - n],
                wrecv.at[3 + parity, n],
            ))
        return out

    def jacobi(table):
        for m in range(8):
            at = cols_r[:, 128 * m:128 * m + 128]
            got = pick_from([lambda r=r: table[r // 8, r % 8:r % 8 + 1, :] for r in range(72)], at)
            coupled = jnp.sum(got * off_r[:, 128 * m:128 * m + 128], axis=0, keepdims=True)
            mine = table[4, m:m + 1, :]
            Y[m:m + 1, :] = mine + omega * (RATN[4, m:m + 1, :] - mine - coupled)

    def coarse(field, cycle):
        ones = jnp.ones((16, 128), bf16)
        along = (((1,), (1,)), ((), ()))
        sums = lax.dot_general(ones, WH[...], along, preferred_element_type=f32)
        sums = sums + lax.dot_general(ones, WL[...], along, preferred_element_type=f32)
        for r in range(3):
            if r < 2:
                part = HOT[8 * r:8 * r + 8, :] * sums[0:8]
            else:
                part = HOT[16:24, :] * sums[0:8]
            if r % 2 == 0:
                kept = part
            if r == 1:
                both = jnp.concatenate([kept, part], axis=0)
                high = both.astype(bf16)
                AB[0:16, :] = high
                AB[32:48, :] = (both - high.astype(f32)).astype(bf16)
            if r == 2:
                both = jnp.concatenate([part, jnp.zeros_like(part)], axis=0)
                high = both.astype(bf16)
                AB[16:32, :] = high
                AB[48:64, :] = (both - high.astype(f32)).astype(bf16)
        listed = jnp.dot(AB[...], LHOT[...], preferred_element_type=f32)
        listed = listed[0:32] + listed[32:64]
        for r in range(18):
            o, h = r // 2, r % 2
            OUT[o // 3, o % 3, h:h + 1, :] = listed[r:r + 1, :]
        step = wide(OUT, ARR, 0, True)
        go(step)
        ARR[2, 2] = OUT[...]
        if cycle == 0:
            land(tables)
        land(step)
        for p in range(9):
            total = jnp.zeros((8, 128), f32)
            for o in range(9):
                at = INVN[p, o]
                sx, sy = p // 3 + o // 3, p % 3 + o % 3
                other = 8 - o
                for h in range(2):
                    got = pick(ARR[sx, sy, other // 3, other % 3, h:h + 1, :], at)
                    total = total + jnp.where((at >> 7) == h, got, 0.0)
            ratio = total * DIAN[p]
            RATN[p] = ratio
            TAB[0, p] = omega * ratio
        jacobi(TAB.at[0])
        for s in range(1, CJ - 1):
            table = TAB.at[s % 2]
            step = around(lambda o: Y, table, csend.at[s % 2], crecv.at[s % 2])
            go(step)
            table[4] = Y[...]
            land(step)
            jacobi(table)
        step = wide(Y, T25, 1, False)
        go(step)
        T25[2, 2] = Y[...]
        land(step)
        for o in range(9):
            BASE[o] = (1.0 - omega) * T25[1 + o // 3, 1 + o % 3] + omega * RATN[o]

        for o in range(9):
            ox, oy = o // 3, o % 3
            for h in range(2):
                at = ENT[o, h, 16:24, :].astype(jnp.int32)
                base = pick_from([lambda r=r: BASE[o, r:r + 1, :] for r in range(8)], at)
                at = ENT[o, h, 0:8, :].astype(jnp.int32)
                got = pick_from(
                    [lambda r=r: T25[ox + r // 24, oy + (r // 8) % 3, r % 8:r % 8 + 1, :] for r in range(72)], at
                )
                coupled = jnp.sum(got * ENT[o, h, 8:16, :], axis=0, keepdims=True)
                LIST[o, h:h + 1, :] = base[0:1, :] - omega * coupled

        for r4 in range(4):
            VT[8 * r4:8 * r4 + 8, :] = pick_from(
                [lambda r=r: LIST[r // 2, r % 2:r % 2 + 1, :] for r in range(18)], SLOT[8 * r4:8 * r4 + 8, :]
            )
        VT[...] = VT[...].T

        def correct(x):
            for t in range(4):
                total = field[x + W, T + 8 * t:T + 8 * t + 8, :]
                for k in range(2):
                    which = jnp.full((8, 128), 16 * k, jnp.int32) + x
                    spread = []
                    for zb in range(4):
                        b0 = (t * 4 + zb) * 8
                        spread.append(
                            jnp.take_along_axis(VT[b0:b0 + 8, :], which, axis=1, mode="promise_in_bounds")
                        )
                    total = total + PR[k, x, 8 * t:8 * t + 8, :] * jnp.concatenate(spread, axis=1)
                field[x + W, T + 8 * t:T + 8 * t + 8, :] = total

        loop(0, NX, correct)

    VT[...] = jnp.zeros_like(VT)
    for cycle in range(CYCLES):
        field = (P0, P2)[cycle]
        if cycle == 0:
            sweep(2, start_from_zero)
            sweep(1, sweep_b_first)
        else:
            exchange_pressure(field, 3, 1)
            sweep(2, functools.partial(sweep_a, field))
            sweep(1, functools.partial(sweep_b, field, field))
        loop(W, W + NX, functools.partial(restrict, field))
        coarse(field, cycle)
        exchange_pressure(field, 2, 0)
        sweep(1, functools.partial(sweep_a, field))
        sweep(0, functools.partial(sweep_b, field, P2))
    back = pltpu.make_async_copy(P2.at[center], out_h, in_sem.at[0])
    back.start()
    back.wait()


def shards(rhs, perm_h, perm_v, prolong, blk_slot, recv_slot, coarse_cols, coarse_off, coarse_diag):
    padded = pltpu.VMEM((2 * W + NX, 2 * T + NY, NZ), f32)
    hbm = pl.BlockSpec(memory_space=pltpu.HBM)
    i32 = jnp.int32
    return pl.pallas_call(
        kernel,
        out_shape=jax.ShapeDtypeStruct(rhs.shape, f32),
        in_specs=[hbm] * 9,
        out_specs=hbm,
        scratch_shapes=[padded] * 10
        + [
            pltpu.VMEM((2, NX, NY, NZ), f32),
            pltpu.VMEM((2, NX, 8, NZ), f32),
            pltpu.VMEM((2, NX + 4, 8, NZ), f32),
            pltpu.VMEM((2, 8, 8, NZ), f32),
            pltpu.VMEM((2, 2, 8, 8, NZ), f32),
            pltpu.VMEM((2, 2, 2, 8, NZ), f32),
            pltpu.VMEM((4096, 128), bf16),
            pltpu.VMEM((4096, 128), bf16),
            pltpu.VMEM((24, 4096), f32),
            pltpu.VMEM((4096, 128), bf16),
            pltpu.VMEM((64, 4096), bf16),
            pltpu.VMEM((32, 128), i32),
            pltpu.VMEM((128, 128), i32),
            pltpu.VMEM((128, 128), f32),
            pltpu.VMEM((24, 128), i32),
            pltpu.VMEM((9, 9, 8, 128), i32),
            pltpu.VMEM((9, 8, 128), f32),
            pltpu.VMEM((9, 2, 24, 128), f32),
            pltpu.VMEM((9, 2, 24, 128), f32),
            pltpu.VMEM((3, 3, 2, 128), f32),
            pltpu.VMEM((5, 5, 3, 3, 2, 128), f32),
            pltpu.VMEM((9, 8, 128), f32),
            pltpu.VMEM((2, 9, 8, 128), f32),
            pltpu.VMEM((5, 5, 8, 128), f32),
            pltpu.VMEM((9, 2, 128), f32),
            pltpu.VMEM((8, 128), f32),
            pltpu.VMEM((9, 8, 128), f32),
            pltpu.VMEM((2, NX, 128), i32),
            pltpu.VMEM((1, 2304), i32),
            pltpu.VMEM((8, 1024), i32),
            pltpu.VMEM((8, 1024), f32),
            pltpu.VMEM((1, 1024), f32),
            pltpu.SemaphoreType.DMA((9,)),
            pltpu.SemaphoreType.DMA((4, 6)),
            pltpu.SemaphoreType.DMA((4, 6)),
            pltpu.SemaphoreType.DMA((2, 4, 2)),
            pltpu.SemaphoreType.DMA((2, 4, 2)),
            pltpu.SemaphoreType.DMA((2, 9)),
            pltpu.SemaphoreType.DMA((2, 9)),
            pltpu.SemaphoreType.DMA((5, 24)),
            pltpu.SemaphoreType.DMA((5, 24)),
        ],
        compiler_params=pltpu.CompilerParams(
            collective_id=0, has_side_effects=True, vmem_limit_bytes=52 << 20
        ),
    )(rhs, perm_h, perm_v, prolong, blk_slot, recv_slot.T, coarse_cols, coarse_off, coarse_diag)


def solution(mesh):
    placed = (
        P("sx", "sy", None),
        P("sx", "sy", None),
        P("sx", "sy", None),
        P(None, "sx", "sy", None),
        P(None, "sx", "sy"),
        P(None, ("sx", "sy")),
        P(None, ("sx", "sy")),
        P(None, ("sx", "sy")),
        P(None, ("sx", "sy")),
    )
    return jax.shard_map(
        shards, mesh=mesh, in_specs=placed, out_specs=P("sx", "sy", None), check_vma=False
    )
```

```python
import functools

import jax
import jax.numpy as jnp
from jax import lax
from jax.experimental import pallas as pl
from jax.experimental.pallas import tpu as pltpu
from jax.sharding import PartitionSpec as P

CYCLES = 2
CJ = 4

storage_coef = 0.01
cheb_low = 0.25
cheb_high = 2.0
omega = 0.8

THETA = 0.5 * (cheb_high + cheb_low)
DELTA = 0.5 * (cheb_high - cheb_low)
SIGMA = THETA / DELTA
RHO0 = 1.0 / SIGMA
RHO1 = 1.0 / (2.0 * SIGMA - RHO0)
ALPHA = RHO1 * RHO0
BETA = 2.0 * RHO1 / DELTA

W = 3
T = 8
NX, NY, NZ = 16, 32, 512
TILES = (NY + 2 * T) // 8
MESH = pl.DeviceIdType.MESH
AROUND = (0, 2, 6, 8, 3, 5, 1, 7)
NEAR = tuple((dx, dy) for dx in range(-2, 3) for dy in range(-2, 3) if (dx, dy) != (0, 0))
f32 = jnp.float32
bf16 = jnp.bfloat16


def neighbour(dx, dy):
    x = lax.axis_index("sx") + dx
    y = lax.axis_index("sy") + dy
    there = (x >= 0) & (x < lax.axis_size("sx")) & (y >= 0) & (y < lax.axis_size("sy"))
    return x, y, there


def inverse(value):
    guess = pl.reciprocal(value, approx=True)
    return guess * (2.0 - value * guess)


def harmonic(left, right):
    total = left + right
    return 2.0 * left * right * inverse(jnp.where(total == 0.0, 1.0, total))


def pick(row, at):
    return jnp.take_along_axis(
        jnp.broadcast_to(row, at.shape), at & 127, axis=1, mode="promise_in_bounds"
    )


def pick_from(table_rows, at):
    high = at >> 7
    got = jnp.zeros(at.shape, f32)
    for r, row in enumerate(table_rows):
        got = jnp.where(high == r, pick(row(), at), got)
    return got


def kernel(
    rhs_h, ph_h, pv_h, pr_h, slot_h, recv_h, cols_h, off_h, diag_h, out_h,
    RHS, PH, PV, TE, TN, TU, INV, P0, P1, P2, PR, PKS, RKS, PKP, RKP, RKC,
    WH, WL, HOT, LHOT, AB, SLOT, LT, VT, RIDX, INVN, DIAN, MSG, ENT,
    OUT, ARR, RATN, TAB, T25, LIST, Y, BASE,
    slot_r, recv_r, cols_r, off_r, diag_r,
    in_sem, fsend, frecv, psend, precv, csend, crecv, wsend, wrecv,
):
    sub = lax.broadcasted_iota(jnp.int32, (8, 128), 0)
    lane = lax.broadcasted_iota(jnp.int32, (8, 128), 1)
    sub512 = lax.broadcasted_iota(jnp.int32, (8, NZ), 0)
    lane512 = lax.broadcasted_iota(jnp.int32, (8, NZ), 1)

    def rows(j):
        return slice(8 * j, 8 * j + 8)

    inner = pl.ds(T, NY)
    center = (pl.ds(W, NX), inner, slice(None))
    loads = [
        pltpu.make_async_copy(src, dst, in_sem.at[n])
        for n, (src, dst) in enumerate(
            [(ph_h, PH.at[center]), (pv_h, PV.at[center]), (rhs_h, RHS.at[center]),
             (slot_h, slot_r), (recv_h, recv_r), (cols_h, cols_r), (off_h, off_r), (diag_h, diag_r),
             (pr_h, PR)]
        )
    ]
    for load in loads:
        load.start()

    bar = pltpu.get_barrier_semaphore()
    for o in AROUND:
        x, y, there = neighbour(o // 3 - 1, o % 3 - 1)

        @pl.when(there)
        def _():
            pl.semaphore_signal(bar, inc=1, device_id=(x, y), device_id_type=MESH)

    def loop(lo, hi, fn):
        pairs = (hi - lo) // 2

        def body(n, carry):
            fn(lo + 2 * n)
            fn(lo + 2 * n + 1)
            return carry

        lax.fori_loop(0, pairs, body, 0)
        if (hi - lo) % 2:
            fn(hi - 1)

    def clear(view):
        def one(i):
            view[i] = jnp.zeros(view.shape[1:], f32)

        loop(0, view.shape[0], one)

    for array in (PH, PV, RHS, P0, P2):
        for dx, strip in ((-1, pl.ds(0, W)), (1, pl.ds(W + NX, W))):
            _, _, there = neighbour(dx, 0)

            @pl.when(jnp.logical_not(there))
            def _():
                clear(array.at[strip])

    for i in (0, 2 * W + NX - 1):
        for j in (0, TILES - 1):
            PH[i, rows(j), :] = jnp.zeros((8, NZ), f32)
    for side, dy in ((0, -1), (1, 1)):
        _, _, there = neighbour(0, dy)

        @pl.when(jnp.logical_not(there))
        def _():
            clear(RKS.at[side])
            clear(P0.at[:, pl.ds(0 if side == 0 else T + NY, T), :])
            clear(P2.at[:, pl.ds(0 if side == 0 else T + NY, T), :])

    for dx, strip in ((-1, pl.ds(0, 2)), (1, pl.ds(NX + 2, 2))):
        _, _, there = neighbour(dx, 0)

        @pl.when(jnp.logical_not(there))
        def _():
            clear(RKS.at[0, strip])
            clear(RKS.at[1, strip])

    for load in loads[:3]:
        load.wait()

    def pack_first(x):
        i = x + W
        a, b, c = PH[i, rows(1), :], PV[i, rows(1), :], RHS[i, rows(1), :]
        PKS[0, x] = jnp.where(sub512 < 3, a, jnp.where(sub512 < 5, pltpu.roll(b, 3, 0), pltpu.roll(c, 5, 0)))
        a, b, c = PH[i, rows(4), :], PV[i, rows(4), :], RHS[i, rows(4), :]
        PKS[1, x] = jnp.where(sub512 >= 5, a, jnp.where(sub512 >= 3, pltpu.roll(b, 5, 0), pltpu.roll(c, 3, 0)))

    loop(0, NX, pack_first)

    peers = sum(neighbour(o // 3 - 1, o % 3 - 1)[2].astype(jnp.int32) for o in AROUND)
    pl.semaphore_wait(bar, peers)

    def go(copies):
        for there, copy, _ in copies:
            @pl.when(there)
            def _():
                copy.start()

    def land(copies):
        for there, copy, arrive in copies:
            @pl.when(there)
            def _():
                arrive.wait_recv()
                copy.wait_send()

    def moved(to, src, there_dst, here_dst, send, recv_there, recv_here):
        x, y, there = neighbour(*to)
        copy = pltpu.make_async_remote_copy(
            src, there_dst, send, recv_there, device_id=(x, y), device_id_type=MESH
        )
        arrive = pltpu.make_async_remote_copy(
            here_dst, here_dst, send, recv_here, device_id=(x, y), device_id_type=MESH
        )
        return there, copy, arrive

    def x_strips(field, src, base, width, send, recv):
        out = []
        for dx in (-1, 1):
            if dx < 0:
                take, put, get = base, W + NX, W - width
            else:
                take, put, get = base + NX - width, W - width, W + NX
            pick_y = inner if base else slice(None)
            out.append(moved(
                (dx, 0), src.at[pl.ds(take, width), pick_y, :], field.at[pl.ds(put, width), inner, :],
                field.at[pl.ds(get, width), inner, :],
                send.at[(dx + 1) // 2], recv.at[(1 - dx) // 2], recv.at[(dx + 1) // 2],
            ))
        return out

    first = []
    for dy in (-1, 1):
        side = (dy + 1) // 2
        for dx in (0, -1, 1):
            src = {0: pl.ds(0, NX), -1: pl.ds(0, 2), 1: pl.ds(NX - 2, 2)}[dx]
            put = {0: pl.ds(2, NX), -1: pl.ds(NX + 2, 2), 1: pl.ds(0, 2)}[dx]
            get = {0: pl.ds(2, NX), -1: pl.ds(0, 2), 1: pl.ds(NX + 2, 2)}[dx]
            first.append(moved(
                (dx, dy), PKS.at[side, src], RKS.at[1 - side, put], RKS.at[side, get],
                fsend.at[3, dx + 1 + 3 * side], frecv.at[3, 1 - dx + 3 * (1 - side)],
                frecv.at[3, dx + 1 + 3 * side],
            ))
    for n, (field, src, width) in enumerate(((PH, ph_h, 3), (PV, pv_h, 2), (RHS, rhs_h, 2))):
        first += x_strips(field, src, 0, width, fsend.at[n], frecv.at[n])
    go(first)

    for load in loads[3:]:
        load.wait()
    for k in range(2):
        for x8 in range(2):
            raw = slot_r[k, 8 * x8:8 * x8 + 8, :]
            order = (((lane >> 5) << 3) + (lane & 7)) * 4 + ((lane >> 3) & 3)
            SLOT[pl.ds(16 * k + 8 * x8, 8), :] = jnp.take_along_axis(
                raw, order, axis=1, mode="promise_in_bounds"
            )
    RIDX[...] = jnp.full_like(RIDX, 1024)
    for r in range(18):
        RIDX[r:r + 1, :] = recv_r[0:1, r * 128:(r + 1) * 128]
    low = lax.broadcasted_iota(jnp.int32, (128, 128), 0)
    cnum = lane.astype(f32) + 1.0
    for o in range(9):
        total = jnp.zeros((8, 128), f32)
        for h in range(2):
            ids = RIDX[2 * o + h:2 * o + h + 1, :]
            a = jnp.where(jnp.broadcast_to(ids >> 7, (8, 128)) == sub, cnum + 128.0 * h, 0.0)
            b = (jnp.broadcast_to(ids & 127, (128, 128)) == low).astype(f32)
            total = total + lax.dot_general(
                a.astype(bf16), b.astype(bf16), (((1,), (1,)), ((), ())),
                preferred_element_type=f32,
            )
        INVN[4, o] = (total + 0.5).astype(jnp.int32) - 1
    for m in range(8):
        DIAN[4, m:m + 1, :] = diag_r[0:1, m * 128:(m + 1) * 128]
    DIAN[4] = 1.0 / DIAN[4]
    for o in range(9):
        for h in range(2):
            at = jnp.broadcast_to(RIDX[2 * o + h:2 * o + h + 1, :], (8, 128))
            at = jnp.where(at == 1024, 0, at)
            cols = jnp.zeros((8, 128), f32)
            offs = jnp.zeros((8, 128), f32)
            for m in range(8):
                piece = slice(128 * m, 128 * m + 128)
                hit = (at >> 7) == m
                cols = jnp.where(hit, pick(cols_r[:, piece].astype(f32), at), cols)
                offs = jnp.where(hit, pick(off_r[:, piece], at), offs)
            MSG[o, h, 0:8, :] = cols
            MSG[o, h, 8:16, :] = offs
            MSG[o, h, 16:24, :] = at.astype(f32)
    ENT[4] = MSG[4]

    def around(src, dst, send, recv):
        out = []
        for o in AROUND:
            out.append(moved(
                (o // 3 - 1, o % 3 - 1), src(o), dst.at[8 - o], dst.at[o],
                send.at[o], recv.at[8 - o], recv.at[o],
            ))
        return out

    tables = []
    for o in AROUND:
        to = (o // 3 - 1, o % 3 - 1)
        tables.append(moved(to, INVN.at[4], INVN.at[8 - o], INVN.at[o], wsend.at[0, o], wrecv.at[0, 8 - o], wrecv.at[0, o]))
        tables.append(moved(to, DIAN.at[4], DIAN.at[8 - o], DIAN.at[o], wsend.at[1, o], wrecv.at[1, 8 - o], wrecv.at[1, o]))
    tables += around(lambda o: MSG.at[o], ENT, wsend.at[2], wrecv.at[2])
    go(tables)

    LT[...] = jnp.zeros_like(LT)
    LT[0:32, :] = SLOT[...] & 127
    LT[...] = LT[...].T
    lane_all = lax.broadcasted_iota(jnp.int32, (128, 128), 1)
    row24 = lax.broadcasted_iota(jnp.int32, (24, 128), 0)
    for kx in range(32):
        line = jnp.broadcast_to(SLOT[kx:kx + 1, :] >> 7, (24, 128))
        HOT[:, kx * 128:(kx + 1) * 128] = (line == row24).astype(f32)
        LHOT[kx * 128:(kx + 1) * 128, :] = (
            jnp.broadcast_to(LT[:, kx:kx + 1], (128, 128)) == lane_all
        ).astype(f32).astype(bf16)
    AB[...] = jnp.zeros_like(AB)

    def edge_x(i, tiles):
        for j in tiles:
            TE[i, rows(j), :] = harmonic(PH[i, rows(j), :], PH[i + 1, rows(j), :])

    def edge_yz(i, new, done):
        for j in new:
            ctr = PH[i, rows(j), :]
            if j < TILES - 1:
                up = PH[i, 8 * j + 1:8 * j + 9, :]
            else:
                up = pltpu.roll(ctr, 7, 0)
            TN[i, rows(j), :] = harmonic(ctr, up)
            pv = PV[i, rows(j), :]
            TU[i, rows(j), :] = jnp.where(
                lane512 == NZ - 1, 0.0, harmonic(pv, pltpu.roll(pv, NZ - 1, 1))
            )
        for j in done:
            tn = TN[i, rows(j), :]
            down = TN[i, 8 * j - 1:8 * j + 7, :] if j > 0 else pltpu.roll(tn, 1, 0)
            tu = TU[i, rows(j), :]
            total = storage_coef + TE[i, rows(j), :] + TE[i - 1, rows(j), :] + tn + down + tu + pltpu.roll(tu, 1, 1)
            INV[i, rows(j), :] = inverse(total)

    every = tuple(range(TILES))
    loop(W, W + NX - 1, lambda i: edge_x(i, (1, 2, 3, 4)))
    loop(W + 1, W + NX - 1, lambda i: edge_yz(i, (1, 2, 3), (2, 3)))

    land(first)

    def unpack_first(i):
        got = RKS[0, i - 1]
        PH[i, rows(0), :] = jnp.where(sub512 >= 5, got, 0.0)
        PV[i, rows(0), :] = jnp.where(sub512 >= 6, pltpu.roll(got, 3, 0), 0.0)
        RHS[i, rows(0), :] = jnp.where(sub512 >= 6, pltpu.roll(got, 5, 0), 0.0)
        got = RKS[1, i - 1]
        PH[i, rows(5), :] = jnp.where(sub512 < 3, got, 0.0)
        PV[i, rows(5), :] = jnp.where(sub512 < 2, pltpu.roll(got, 5, 0), 0.0)
        RHS[i, rows(5), :] = jnp.where(sub512 < 2, pltpu.roll(got, 3, 0), 0.0)

    loop(1, NX + 5, unpack_first)
    for lo, hi in ((0, W), (W + NX - 1, 2 * W + NX - 1)):
        loop(lo, hi, lambda i: edge_x(i, every))
    loop(W, W + NX - 1, lambda i: edge_x(i, (0, 5)))
    for lo, hi in ((1, W + 1), (W + NX - 1, 2 * W + NX - 1)):
        loop(lo, hi, lambda i: edge_yz(i, every, every))
    loop(W + 1, W + NX - 1, lambda i: edge_yz(i, (0, 4, 5), (0, 1, 4, 5)))

    def residuals(field, i, tiles):
        before = None
        for j in tiles:
            ctr = field[i, rows(j), :]
            acc = RHS[i, rows(j), :] - storage_coef * ctr
            acc = acc + TE[i, rows(j), :] * (field[i + 1, rows(j), :] - ctr)
            acc = acc + TE[i - 1, rows(j), :] * (field[i - 1, rows(j), :] - ctr)
            fz = TU[i, rows(j), :] * (pltpu.roll(ctr, NZ - 1, 1) - ctr)
            acc = acc + fz - pltpu.roll(fz, 1, 1)
            up = pltpu.roll(ctr, 7, 0)
            if j < TILES - 1:
                up = jnp.where(sub512 == 7, pltpu.roll(field[i, rows(j + 1), :], 7, 0), up)
            fn = TN[i, rows(j), :] * (up - ctr)
            turned = pltpu.roll(fn, 1, 0)
            if before is not None:
                fs = jnp.where(sub512 == 0, before, turned)
            elif j > 0:
                fs = TN[i, 8 * j - 1:8 * j + 7, :] * (ctr - field[i, 8 * j - 1:8 * j + 7, :])
            else:
                fs = turned
            before = turned
            yield j, ctr, acc + fn - fs

    def sweep(extent, update):
        tiles = tuple(range(TILES)) if extent > 0 else tuple(range(1, TILES - 1))
        loop(W - extent, W + NX + extent, lambda i: update(i, tiles))

    def start_from_zero(i, tiles):
        for j in tiles:
            P1[i, rows(j), :] = (1.0 / THETA) * INV[i, rows(j), :] * RHS[i, rows(j), :]

    def sweep_a(field, i, tiles):
        for j, ctr, res in residuals(field, i, tiles):
            P1[i, rows(j), :] = ctr + (1.0 / THETA) * INV[i, rows(j), :] * res

    def sweep_b_first(i, tiles):
        for j, ctr, res in residuals(P1, i, tiles):
            P0[i, rows(j), :] = (1.0 + ALPHA) * ctr + BETA * INV[i, rows(j), :] * res

    def sweep_b(old, new, i, tiles):
        for j, ctr, res in residuals(P1, i, tiles):
            new[i, rows(j), :] = (1.0 + ALPHA) * ctr - ALPHA * old[i, rows(j), :] + BETA * INV[i, rows(j), :] * res

    def exchange_pressure(field, width, slot, meanwhile=None):
        per = 8 // (2 if width == 2 else 4)
        span = 8 // per
        tiles = NX // per

        def pack(g):
            a = b = None
            for m in range(per):
                i = W + g * per + m
                one = field[i, rows(1), :]
                two = field[i, rows(4), :]
                one = one if m == 0 else pltpu.roll(one, m * span, 0)
                two = two if (m + 1) * span == 8 else pltpu.roll(two, (m + 1) * span, 0)
                a = one if a is None else jnp.where(sub512 >= m * span, one, a)
                b = two if b is None else jnp.where(sub512 >= m * span, two, b)
            PKP[0, g] = a
            PKP[1, g] = b

        loop(0, tiles, pack)
        step = x_strips(field, field, W, width, psend.at[slot, 0], precv.at[slot, 0])
        for dy in (-1, 1):
            side = (dy + 1) // 2
            step.append(moved(
                (0, dy), PKP.at[side, pl.ds(0, tiles)], RKP.at[slot, 1 - side, pl.ds(0, tiles)],
                RKP.at[slot, side, pl.ds(0, tiles)],
                psend.at[slot, 1, side], precv.at[slot, 1, 1 - side], precv.at[slot, 1, side],
            ))
            for dx in (-1, 1):
                far = (dx + 1) // 2
                step.append(moved(
                    (dx, dy), PKP.at[side, 0 if dx < 0 else tiles - 1], RKC.at[slot, 1 - side, 1 - far],
                    RKC.at[slot, side, far],
                    psend.at[slot, 2 + side, far], precv.at[slot, 2 + 1 - side, 1 - far], precv.at[slot, 2 + side, far],
                ))
        go(step)
        if meanwhile is not None:
            meanwhile()
        land(step)

        def place(side, tile, m, i):
            if side == 0:
                turn = (8 - span - m * span) % 8
            else:
                turn = (-m * span) % 8
            tile = pltpu.roll(tile, turn, 0) if turn else tile
            field[i, rows(0 if side == 0 else 5), :] = tile

        for side, dy in ((0, -1), (1, 1)):
            _, _, there = neighbour(0, dy)

            @pl.when(there)
            def _():
                def body(g):
                    tile = RKP[slot, side, g]
                    for m in range(per):
                        place(side, tile, m, W + g * per + m)

                loop(0, tiles, body)

            for far, dx in ((0, -1), (1, 1)):
                _, _, there = neighbour(dx, dy)

                @pl.when(there)
                def _():
                    tile = RKC[slot, side, far]
                    for depth in range(width - 1):
                        if dx < 0:
                            place(side, tile, per - 1 - depth, W - 1 - depth)
                        else:
                            place(side, tile, depth, W + NX + depth)

    def restrict(field, i):
        x = i - W
        for j, _, res in residuals(field, i, tuple(range(1, TILES - 1))):
            t = j - 1
            for k in range(2):
                scaled = PR[k, x, 8 * t:8 * t + 8, :] * res
                for h in range(2):
                    both = jnp.concatenate(
                        [scaled[:, 256 * h:256 * h + 128], scaled[:, 256 * h + 128:256 * h + 256]], axis=0
                    )
                    high = both.astype(bf16)
                    at = pl.multiple_of((16 * k + x) * 128 + (t * 4 + 2 * h) * 8, 16)
                    WH[pl.ds(at, 16), :] = high
                    WL[pl.ds(at, 16), :] = (both - high.astype(f32)).astype(bf16)

    def wide(src, dst, parity, lists):
        out = []
        for n, (dx, dy) in enumerate(NEAR):
            if lists:
                def rect(ax, ay):
                    x0, x1 = max(-1, ax - 1) + 1, min(1, ax + 1) + 2
                    y0, y1 = max(-1, ay - 1) + 1, min(1, ay + 1) + 2
                    return pl.ds(x0, x1 - x0), pl.ds(y0, y1 - y0)
                give, take = rect(dx, dy), rect(-dx, -dy)
                piece, put, get = src.at[give], dst.at[(2 - dx, 2 - dy) + give], dst.at[(2 + dx, 2 + dy) + take]
            else:
                piece, put, get = src, dst.at[2 - dx, 2 - dy], dst.at[2 + dx, 2 + dy]
            out.append(((2 * abs(dy) + abs(dx)), moved(
                (dx, dy), piece, put, get, wsend.at[3 + parity, n], wrecv.at[3 + parity, 23 - n],
                wrecv.at[3 + parity, n],
            )))
        return [entry for _, entry in sorted(out, key=lambda pair: -pair[0])]

    def jacobi(table):
        for m in range(8):
            at = cols_r[:, 128 * m:128 * m + 128]
            got = pick_from([lambda r=r: table[r // 8, r % 8:r % 8 + 1, :] for r in range(72)], at)
            coupled = jnp.sum(got * off_r[:, 128 * m:128 * m + 128], axis=0, keepdims=True)
            mine = table[4, m:m + 1, :]
            Y[m:m + 1, :] = mine + omega * (RATN[4, m:m + 1, :] - mine - coupled)

    def coarse(field, cycle):
        ones = jnp.ones((16, 128), bf16)
        along = (((1,), (1,)), ((), ()))
        sums = lax.dot_general(ones, WH[...], along, preferred_element_type=f32)
        sums = sums + lax.dot_general(ones, WL[...], along, preferred_element_type=f32)
        for r in range(3):
            if r < 2:
                part = HOT[8 * r:8 * r + 8, :] * sums[0:8]
            else:
                part = HOT[16:24, :] * sums[0:8]
            if r % 2 == 0:
                kept = part
            if r == 1:
                both = jnp.concatenate([kept, part], axis=0)
                high = both.astype(bf16)
                AB[0:16, :] = high
                AB[32:48, :] = (both - high.astype(f32)).astype(bf16)
            if r == 2:
                both = jnp.concatenate([part, jnp.zeros_like(part)], axis=0)
                high = both.astype(bf16)
                AB[16:32, :] = high
                AB[48:64, :] = (both - high.astype(f32)).astype(bf16)
        listed = jnp.dot(AB[...], LHOT[...], preferred_element_type=f32)
        listed = listed[0:32] + listed[32:64]
        for r in range(18):
            o, h = r // 2, r % 2
            OUT[o // 3, o % 3, h:h + 1, :] = listed[r:r + 1, :]
        step = wide(OUT, ARR, 0, True)
        go(step)
        ARR[2, 2] = OUT[...]
        if cycle == 0:
            land(tables)
        land(step)
        for p in range(9):
            total = jnp.zeros((8, 128), f32)
            for o in range(9):
                at = INVN[p, o]
                sx, sy = p // 3 + o // 3, p % 3 + o % 3
                other = 8 - o
                for h in range(2):
                    got = pick(ARR[sx, sy, other // 3, other % 3, h:h + 1, :], at)
                    total = total + jnp.where((at >> 7) == h, got, 0.0)
            ratio = total * DIAN[p]
            RATN[p] = ratio
            TAB[0, p] = omega * ratio
        jacobi(TAB.at[0])
        for s in range(1, CJ - 1):
            table = TAB.at[s % 2]
            step = around(lambda o: Y, table, csend.at[s % 2], crecv.at[s % 2])
            go(step)
            table[4] = Y[...]
            land(step)
            jacobi(table)
        step = wide(Y, T25, 1, False)
        go(step)
        T25[2, 2] = Y[...]
        land(step)
        for o in range(9):
            BASE[o] = (1.0 - omega) * T25[1 + o // 3, 1 + o % 3] + omega * RATN[o]

        for o in range(9):
            ox, oy = o // 3, o % 3
            at = jnp.concatenate([ENT[o, h, 16:24, :] for h in range(2)], axis=0).astype(jnp.int32)
            base = pick_from([lambda r=r: BASE[o, r:r + 1, :] for r in range(8)], at)
            at = jnp.concatenate([ENT[o, h, 0:8, :] for h in range(2)], axis=0).astype(jnp.int32)
            got = pick_from(
                [lambda r=r: T25[ox + r // 24, oy + (r // 8) % 3, r % 8:r % 8 + 1, :] for r in range(72)], at
            )
            for h in range(2):
                coupled = jnp.sum(got[8 * h:8 * h + 8] * ENT[o, h, 8:16, :], axis=0, keepdims=True)
                LIST[o, h:h + 1, :] = base[8 * h:8 * h + 1, :] - omega * coupled

        for r4 in range(4):
            VT[8 * r4:8 * r4 + 8, :] = pick_from(
                [lambda r=r: LIST[r // 2, r % 2:r % 2 + 1, :] for r in range(18)], SLOT[8 * r4:8 * r4 + 8, :]
            )
        VT[...] = VT[...].T

        def correct(x, blocks):
            for t in blocks:
                total = field[x + W, T + 8 * t:T + 8 * t + 8, :]
                for k in range(2):
                    which = jnp.full((8, 128), 16 * k, jnp.int32) + x
                    spread = []
                    for zb in range(4):
                        b0 = (t * 4 + zb) * 8
                        spread.append(
                            jnp.take_along_axis(VT[b0:b0 + 8, :], which, axis=1, mode="promise_in_bounds")
                        )
                    total = total + PR[k, x, 8 * t:8 * t + 8, :] * jnp.concatenate(spread, axis=1)
                field[x + W, T + 8 * t:T + 8 * t + 8, :] = total

        for lo in (0, NX - 2):
            correct(lo, range(4))
            correct(lo + 1, range(4))
        loop(2, NX - 2, lambda x: correct(x, (0, 3)))
        return lambda: loop(2, NX - 2, lambda x: correct(x, (1, 2)))

    VT[...] = jnp.zeros_like(VT)
    for cycle in range(CYCLES):
        field = (P0, P2)[cycle]
        if cycle == 0:
            sweep(2, start_from_zero)
            sweep(1, sweep_b_first)
        else:
            exchange_pressure(field, 3, 1)
            sweep(2, functools.partial(sweep_a, field))
            sweep(1, functools.partial(sweep_b, field, field))
        loop(W, W + NX, functools.partial(restrict, field))
        rest = coarse(field, cycle)
        exchange_pressure(field, 2, 0, rest)
        sweep(1, functools.partial(sweep_a, field))
        sweep(0, functools.partial(sweep_b, field, P2))
    back = pltpu.make_async_copy(P2.at[center], out_h, in_sem.at[0])
    back.start()
    back.wait()


def shards(rhs, perm_h, perm_v, prolong, blk_slot, recv_slot, coarse_cols, coarse_off, coarse_diag):
    padded = pltpu.VMEM((2 * W + NX, 2 * T + NY, NZ), f32)
    hbm = pl.BlockSpec(memory_space=pltpu.HBM)
    i32 = jnp.int32
    return pl.pallas_call(
        kernel,
        out_shape=jax.ShapeDtypeStruct(rhs.shape, f32),
        in_specs=[hbm] * 9,
        out_specs=hbm,
        scratch_shapes=[padded] * 10
        + [
            pltpu.VMEM((2, NX, NY, NZ), f32),
            pltpu.VMEM((2, NX, 8, NZ), f32),
            pltpu.VMEM((2, NX + 4, 8, NZ), f32),
            pltpu.VMEM((2, 8, 8, NZ), f32),
            pltpu.VMEM((2, 2, 8, 8, NZ), f32),
            pltpu.VMEM((2, 2, 2, 8, NZ), f32),
            pltpu.VMEM((4096, 128), bf16),
            pltpu.VMEM((4096, 128), bf16),
            pltpu.VMEM((24, 4096), f32),
            pltpu.VMEM((4096, 128), bf16),
            pltpu.VMEM((64, 4096), bf16),
            pltpu.VMEM((32, 128), i32),
            pltpu.VMEM((128, 128), i32),
            pltpu.VMEM((128, 128), f32),
            pltpu.VMEM((24, 128), i32),
            pltpu.VMEM((9, 9, 8, 128), i32),
            pltpu.VMEM((9, 8, 128), f32),
            pltpu.VMEM((9, 2, 24, 128), f32),
            pltpu.VMEM((9, 2, 24, 128), f32),
            pltpu.VMEM((3, 3, 2, 128), f32),
            pltpu.VMEM((5, 5, 3, 3, 2, 128), f32),
            pltpu.VMEM((9, 8, 128), f32),
            pltpu.VMEM((2, 9, 8, 128), f32),
            pltpu.VMEM((5, 5, 8, 128), f32),
            pltpu.VMEM((9, 2, 128), f32),
            pltpu.VMEM((8, 128), f32),
            pltpu.VMEM((9, 8, 128), f32),
            pltpu.VMEM((2, NX, 128), i32),
            pltpu.VMEM((1, 2304), i32),
            pltpu.VMEM((8, 1024), i32),
            pltpu.VMEM((8, 1024), f32),
            pltpu.VMEM((1, 1024), f32),
            pltpu.SemaphoreType.DMA((9,)),
            pltpu.SemaphoreType.DMA((4, 6)),
            pltpu.SemaphoreType.DMA((4, 6)),
            pltpu.SemaphoreType.DMA((2, 4, 2)),
            pltpu.SemaphoreType.DMA((2, 4, 2)),
            pltpu.SemaphoreType.DMA((2, 9)),
            pltpu.SemaphoreType.DMA((2, 9)),
            pltpu.SemaphoreType.DMA((5, 24)),
            pltpu.SemaphoreType.DMA((5, 24)),
        ],
        compiler_params=pltpu.CompilerParams(
            collective_id=0, has_side_effects=True, vmem_limit_bytes=63 << 20
        ),
    )(rhs, perm_h, perm_v, prolong, blk_slot, recv_slot.T, coarse_cols, coarse_off, coarse_diag)


def solution(mesh):
    placed = (
        P("sx", "sy", None),
        P("sx", "sy", None),
        P("sx", "sy", None),
        P(None, "sx", "sy", None),
        P(None, "sx", "sy"),
        P(None, ("sx", "sy")),
        P(None, ("sx", "sy")),
        P(None, ("sx", "sy")),
        P(None, ("sx", "sy")),
    )
    return jax.shard_map(
        shards, mesh=mesh, in_specs=placed, out_specs=P("sx", "sy", None), check_vma=False
    )
```

```python
import functools

import jax
import jax.numpy as jnp
from jax import lax
from jax.experimental import pallas as pl
from jax.experimental.pallas import tpu as pltpu
from jax.sharding import PartitionSpec as P

CYCLES = 2
CJ = 4

storage_coef = 0.01
cheb_low = 0.25
cheb_high = 2.0
omega = 0.8

THETA = 0.5 * (cheb_high + cheb_low)
DELTA = 0.5 * (cheb_high - cheb_low)
SIGMA = THETA / DELTA
RHO0 = 1.0 / SIGMA
RHO1 = 1.0 / (2.0 * SIGMA - RHO0)
ALPHA = RHO1 * RHO0
BETA = 2.0 * RHO1 / DELTA

W = 3
T = 8
NX, NY, NZ = 16, 32, 512
TILES = (NY + 2 * T) // 8
MESH = pl.DeviceIdType.MESH
AROUND = (0, 2, 6, 8, 3, 5, 1, 7)
NEAR = tuple((dx, dy) for dx in range(-2, 3) for dy in range(-2, 3) if (dx, dy) != (0, 0))
f32 = jnp.float32
bf16 = jnp.bfloat16


def neighbour(dx, dy):
    x = lax.axis_index("sx") + dx
    y = lax.axis_index("sy") + dy
    there = (x >= 0) & (x < lax.axis_size("sx")) & (y >= 0) & (y < lax.axis_size("sy"))
    return x, y, there


def inverse(value):
    guess = pl.reciprocal(value, approx=True)
    return guess * (2.0 - value * guess)


def harmonic(left, right):
    total = left + right
    return 2.0 * left * right * inverse(jnp.where(total == 0.0, 1.0, total))


def pick(row, at):
    return jnp.take_along_axis(
        jnp.broadcast_to(row, at.shape), at & 127, axis=1, mode="promise_in_bounds"
    )


def pick_from(table_rows, at, got=None, chosen=None):
    high = at >> 7
    got = jnp.zeros(at.shape, f32) if got is None else got
    for r, row in enumerate(table_rows):
        if chosen is None or r in chosen:
            got = jnp.where(high == r, pick(row(), at), got)
    return got


def kernel(
    rhs_h, ph_h, pv_h, pr_h, slot_h, recv_h, cols_h, off_h, diag_h, out_h,
    RHS, PH, PV, TE, TN, TU, INV, P0, P1, P2, PR, PKS, RKS, PKP, RKP, RKC,
    WH, WL, HOT, LHOT, AB, SLOT, LT, VT, RIDX, INVN, DIAN, MSG, ENT,
    OUT, ARR, RATN, TAB, T25, LIST, Y, BASE, LASTB, LASTG,
    slot_r, recv_r, cols_r, off_r, diag_r,
    in_sem, fsend, frecv, psend, precv, csend, crecv, wsend, wrecv,
):
    sub = lax.broadcasted_iota(jnp.int32, (8, 128), 0)
    lane = lax.broadcasted_iota(jnp.int32, (8, 128), 1)
    sub512 = lax.broadcasted_iota(jnp.int32, (8, NZ), 0)
    lane512 = lax.broadcasted_iota(jnp.int32, (8, NZ), 1)

    def rows(j):
        return slice(8 * j, 8 * j + 8)

    inner = pl.ds(T, NY)
    center = (pl.ds(W, NX), inner, slice(None))
    loads = [
        pltpu.make_async_copy(src, dst, in_sem.at[n])
        for n, (src, dst) in enumerate(
            [(ph_h, PH.at[center]), (pv_h, PV.at[center]), (rhs_h, RHS.at[center]),
             (slot_h, slot_r), (recv_h, recv_r), (cols_h, cols_r), (off_h, off_r), (diag_h, diag_r),
             (pr_h, PR)]
        )
    ]
    for load in loads:
        load.start()

    bar = pltpu.get_barrier_semaphore()
    for o in AROUND:
        x, y, there = neighbour(o // 3 - 1, o % 3 - 1)

        @pl.when(there)
        def _():
            pl.semaphore_signal(bar, inc=1, device_id=(x, y), device_id_type=MESH)

    def loop(lo, hi, fn):
        pairs = (hi - lo) // 2

        def body(n, carry):
            fn(lo + 2 * n)
            fn(lo + 2 * n + 1)
            return carry

        lax.fori_loop(0, pairs, body, 0)
        if (hi - lo) % 2:
            fn(hi - 1)

    def clear(view):
        def one(i):
            view[i] = jnp.zeros(view.shape[1:], f32)

        loop(0, view.shape[0], one)

    for array in (PH, PV, RHS, P0, P2):
        for dx, strip in ((-1, pl.ds(0, W)), (1, pl.ds(W + NX, W))):
            _, _, there = neighbour(dx, 0)

            @pl.when(jnp.logical_not(there))
            def _():
                clear(array.at[strip])

    for i in (0, 2 * W + NX - 1):
        for j in (0, TILES - 1):
            PH[i, rows(j), :] = jnp.zeros((8, NZ), f32)
    for side, dy in ((0, -1), (1, 1)):
        _, _, there = neighbour(0, dy)

        @pl.when(jnp.logical_not(there))
        def _():
            clear(RKS.at[side])
            clear(P0.at[:, pl.ds(0 if side == 0 else T + NY, T), :])
            clear(P2.at[:, pl.ds(0 if side == 0 else T + NY, T), :])

    for dx, strip in ((-1, pl.ds(0, 2)), (1, pl.ds(NX + 2, 2))):
        _, _, there = neighbour(dx, 0)

        @pl.when(jnp.logical_not(there))
        def _():
            clear(RKS.at[0, strip])
            clear(RKS.at[1, strip])

    for load in loads[:3]:
        load.wait()

    def pack_first(x):
        i = x + W
        a, b, c = PH[i, rows(1), :], PV[i, rows(1), :], RHS[i, rows(1), :]
        PKS[0, x] = jnp.where(sub512 < 3, a, jnp.where(sub512 < 5, pltpu.roll(b, 3, 0), pltpu.roll(c, 5, 0)))
        a, b, c = PH[i, rows(4), :], PV[i, rows(4), :], RHS[i, rows(4), :]
        PKS[1, x] = jnp.where(sub512 >= 5, a, jnp.where(sub512 >= 3, pltpu.roll(b, 5, 0), pltpu.roll(c, 3, 0)))

    loop(0, NX, pack_first)

    peers = sum(neighbour(o // 3 - 1, o % 3 - 1)[2].astype(jnp.int32) for o in AROUND)
    pl.semaphore_wait(bar, peers)

    def go(copies):
        for there, copy, _ in copies:
            @pl.when(there)
            def _():
                copy.start()

    def land(copies):
        for there, copy, arrive in copies:
            @pl.when(there)
            def _():
                arrive.wait_recv()
                copy.wait_send()

    def moved(to, src, there_dst, here_dst, send, recv_there, recv_here):
        x, y, there = neighbour(*to)
        copy = pltpu.make_async_remote_copy(
            src, there_dst, send, recv_there, device_id=(x, y), device_id_type=MESH
        )
        arrive = pltpu.make_async_remote_copy(
            here_dst, here_dst, send, recv_here, device_id=(x, y), device_id_type=MESH
        )
        return there, copy, arrive

    def x_strips(field, src, base, width, send, recv):
        out = []
        for dx in (-1, 1):
            if dx < 0:
                take, put, get = base, W + NX, W - width
            else:
                take, put, get = base + NX - width, W - width, W + NX
            pick_y = inner if base else slice(None)
            out.append(moved(
                (dx, 0), src.at[pl.ds(take, width), pick_y, :], field.at[pl.ds(put, width), inner, :],
                field.at[pl.ds(get, width), inner, :],
                send.at[(dx + 1) // 2], recv.at[(1 - dx) // 2], recv.at[(dx + 1) // 2],
            ))
        return out

    first = []
    for dy in (-1, 1):
        side = (dy + 1) // 2
        for dx in (0, -1, 1):
            src = {0: pl.ds(0, NX), -1: pl.ds(0, 2), 1: pl.ds(NX - 2, 2)}[dx]
            put = {0: pl.ds(2, NX), -1: pl.ds(NX + 2, 2), 1: pl.ds(0, 2)}[dx]
            get = {0: pl.ds(2, NX), -1: pl.ds(0, 2), 1: pl.ds(NX + 2, 2)}[dx]
            first.append(moved(
                (dx, dy), PKS.at[side, src], RKS.at[1 - side, put], RKS.at[side, get],
                fsend.at[3, dx + 1 + 3 * side], frecv.at[3, 1 - dx + 3 * (1 - side)],
                frecv.at[3, dx + 1 + 3 * side],
            ))
    for n, (field, src, width) in enumerate(((PH, ph_h, 3), (PV, pv_h, 2), (RHS, rhs_h, 2))):
        first += x_strips(field, src, 0, width, fsend.at[n], frecv.at[n])
    go(first)

    for load in loads[3:]:
        load.wait()
    for k in range(2):
        for x8 in range(2):
            raw = slot_r[k, 8 * x8:8 * x8 + 8, :]
            order = (((lane >> 5) << 3) + (lane & 7)) * 4 + ((lane >> 3) & 3)
            SLOT[pl.ds(16 * k + 8 * x8, 8), :] = jnp.take_along_axis(
                raw, order, axis=1, mode="promise_in_bounds"
            )
    RIDX[...] = jnp.full_like(RIDX, 1024)
    for r in range(18):
        RIDX[r:r + 1, :] = recv_r[0:1, r * 128:(r + 1) * 128]
    low = lax.broadcasted_iota(jnp.int32, (128, 128), 0)
    cnum = lane.astype(f32) + 1.0
    for o in range(9):
        total = jnp.zeros((8, 128), f32)
        for h in range(2):
            ids = RIDX[2 * o + h:2 * o + h + 1, :]
            a = jnp.where(jnp.broadcast_to(ids >> 7, (8, 128)) == sub, cnum + 128.0 * h, 0.0)
            b = (jnp.broadcast_to(ids & 127, (128, 128)) == low).astype(f32)
            total = total + lax.dot_general(
                a.astype(bf16), b.astype(bf16), (((1,), (1,)), ((), ())),
                preferred_element_type=f32,
            )
        INVN[4, o] = (total + 0.5).astype(jnp.int32) - 1
    for m in range(8):
        DIAN[4, m:m + 1, :] = diag_r[0:1, m * 128:(m + 1) * 128]
    DIAN[4] = 1.0 / DIAN[4]
    for o in range(9):
        for h in range(2):
            at = jnp.broadcast_to(RIDX[2 * o + h:2 * o + h + 1, :], (8, 128))
            at = jnp.where(at == 1024, 0, at)
            cols = jnp.zeros((8, 128), f32)
            offs = jnp.zeros((8, 128), f32)
            for m in range(8):
                piece = slice(128 * m, 128 * m + 128)
                hit = (at >> 7) == m
                cols = jnp.where(hit, pick(cols_r[:, piece].astype(f32), at), cols)
                offs = jnp.where(hit, pick(off_r[:, piece], at), offs)
            MSG[o, h, 0:8, :] = cols
            MSG[o, h, 8:16, :] = offs
            MSG[o, h, 16:24, :] = at.astype(f32)
    ENT[4] = MSG[4]

    def around(src, dst, send, recv):
        out = []
        for o in AROUND:
            out.append(moved(
                (o // 3 - 1, o % 3 - 1), src(o), dst.at[8 - o], dst.at[o],
                send.at[o], recv.at[8 - o], recv.at[o],
            ))
        return out

    tables = []
    for o in AROUND:
        to = (o // 3 - 1, o % 3 - 1)
        tables.append(moved(to, INVN.at[4], INVN.at[8 - o], INVN.at[o], wsend.at[0, o], wrecv.at[0, 8 - o], wrecv.at[0, o]))
        tables.append(moved(to, DIAN.at[4], DIAN.at[8 - o], DIAN.at[o], wsend.at[1, o], wrecv.at[1, 8 - o], wrecv.at[1, o]))
    tables += around(lambda o: MSG.at[o], ENT, wsend.at[2], wrecv.at[2])

    LT[...] = jnp.zeros_like(LT)
    LT[0:32, :] = SLOT[...] & 127
    LT[...] = LT[...].T
    lane_all = lax.broadcasted_iota(jnp.int32, (128, 128), 1)
    row24 = lax.broadcasted_iota(jnp.int32, (24, 128), 0)
    for kx in range(32):
        line = jnp.broadcast_to(SLOT[kx:kx + 1, :] >> 7, (24, 128))
        HOT[:, kx * 128:(kx + 1) * 128] = (line == row24).astype(f32)
        LHOT[kx * 128:(kx + 1) * 128, :] = (
            jnp.broadcast_to(LT[:, kx:kx + 1], (128, 128)) == lane_all
        ).astype(f32).astype(bf16)
    AB[...] = jnp.zeros_like(AB)

    def edge_x(i, tiles):
        for j in tiles:
            TE[i, rows(j), :] = harmonic(PH[i, rows(j), :], PH[i + 1, rows(j), :])

    def edge_yz(i, new, done):
        for j in new:
            ctr = PH[i, rows(j), :]
            if j < TILES - 1:
                up = PH[i, 8 * j + 1:8 * j + 9, :]
            else:
                up = pltpu.roll(ctr, 7, 0)
            TN[i, rows(j), :] = harmonic(ctr, up)
            pv = PV[i, rows(j), :]
            TU[i, rows(j), :] = jnp.where(
                lane512 == NZ - 1, 0.0, harmonic(pv, pltpu.roll(pv, NZ - 1, 1))
            )
        for j in done:
            tn = TN[i, rows(j), :]
            down = TN[i, 8 * j - 1:8 * j + 7, :] if j > 0 else pltpu.roll(tn, 1, 0)
            tu = TU[i, rows(j), :]
            total = storage_coef + TE[i, rows(j), :] + TE[i - 1, rows(j), :] + tn + down + tu + pltpu.roll(tu, 1, 1)
            inv = inverse(total)
            INV[i, rows(j), :] = inv
            P1[i, rows(j), :] = (1.0 / THETA) * inv * RHS[i, rows(j), :]

    every = tuple(range(TILES))
    loop(W, W + NX - 1, lambda i: edge_x(i, (1, 2, 3, 4)))
    loop(W + 1, W + NX - 1, lambda i: edge_yz(i, (1, 2, 3), (2, 3)))

    land(first)
    go(tables)

    def unpack_first(i):
        got = RKS[0, i - 1]
        PH[i, rows(0), :] = jnp.where(sub512 >= 5, got, 0.0)
        PV[i, rows(0), :] = jnp.where(sub512 >= 6, pltpu.roll(got, 3, 0), 0.0)
        RHS[i, rows(0), :] = jnp.where(sub512 >= 6, pltpu.roll(got, 5, 0), 0.0)
        got = RKS[1, i - 1]
        PH[i, rows(5), :] = jnp.where(sub512 < 3, got, 0.0)
        PV[i, rows(5), :] = jnp.where(sub512 < 2, pltpu.roll(got, 5, 0), 0.0)
        RHS[i, rows(5), :] = jnp.where(sub512 < 2, pltpu.roll(got, 3, 0), 0.0)

    loop(1, NX + 5, unpack_first)
    for lo, hi in ((0, W), (W + NX - 1, 2 * W + NX - 1)):
        loop(lo, hi, lambda i: edge_x(i, every))
    loop(W, W + NX - 1, lambda i: edge_x(i, (0, 5)))
    for lo, hi in ((1, W + 1), (W + NX - 1, 2 * W + NX - 1)):
        loop(lo, hi, lambda i: edge_yz(i, every, every))
    loop(W + 1, W + NX - 1, lambda i: edge_yz(i, (0, 4, 5), (0, 1, 4, 5)))

    def residuals(field, i, tiles):
        before = None
        for j in tiles:
            ctr = field[i, rows(j), :]
            acc = RHS[i, rows(j), :] - storage_coef * ctr
            acc = acc + TE[i, rows(j), :] * (field[i + 1, rows(j), :] - ctr)
            acc = acc + TE[i - 1, rows(j), :] * (field[i - 1, rows(j), :] - ctr)
            fz = TU[i, rows(j), :] * (pltpu.roll(ctr, NZ - 1, 1) - ctr)
            acc = acc + fz - pltpu.roll(fz, 1, 1)
            up = pltpu.roll(ctr, 7, 0)
            if j < TILES - 1:
                up = jnp.where(sub512 == 7, pltpu.roll(field[i, rows(j + 1), :], 7, 0), up)
            fn = TN[i, rows(j), :] * (up - ctr)
            turned = pltpu.roll(fn, 1, 0)
            if before is not None:
                fs = jnp.where(sub512 == 0, before, turned)
            elif j > 0:
                fs = TN[i, 8 * j - 1:8 * j + 7, :] * (ctr - field[i, 8 * j - 1:8 * j + 7, :])
            else:
                fs = turned
            before = turned
            yield j, ctr, acc + fn - fs

    def sweep(extent, update):
        tiles = tuple(range(TILES)) if extent > 0 else tuple(range(1, TILES - 1))
        loop(W - extent, W + NX + extent, lambda i: update(i, tiles))

    def sweep_a(field, i, tiles):
        for j, ctr, res in residuals(field, i, tiles):
            P1[i, rows(j), :] = ctr + (1.0 / THETA) * INV[i, rows(j), :] * res

    def sweep_b_first(i, tiles):
        for j, ctr, res in residuals(P1, i, tiles):
            P0[i, rows(j), :] = (1.0 + ALPHA) * ctr + BETA * INV[i, rows(j), :] * res

    def sweep_b(old, new, i, tiles):
        for j, ctr, res in residuals(P1, i, tiles):
            new[i, rows(j), :] = (1.0 + ALPHA) * ctr - ALPHA * old[i, rows(j), :] + BETA * INV[i, rows(j), :] * res

    def exchange_pressure(field, width, slot, meanwhile=None):
        per = 8 // (2 if width == 2 else 4)
        span = 8 // per
        tiles = NX // per

        def pack(g):
            a = b = None
            for m in range(per):
                i = W + g * per + m
                one = field[i, rows(1), :]
                two = field[i, rows(4), :]
                one = one if m == 0 else pltpu.roll(one, m * span, 0)
                two = two if (m + 1) * span == 8 else pltpu.roll(two, (m + 1) * span, 0)
                a = one if a is None else jnp.where(sub512 >= m * span, one, a)
                b = two if b is None else jnp.where(sub512 >= m * span, two, b)
            PKP[0, g] = a
            PKP[1, g] = b

        loop(0, tiles, pack)
        step = x_strips(field, field, W, width, psend.at[slot, 0], precv.at[slot, 0])
        for dy in (-1, 1):
            side = (dy + 1) // 2
            step.append(moved(
                (0, dy), PKP.at[side, pl.ds(0, tiles)], RKP.at[slot, 1 - side, pl.ds(0, tiles)],
                RKP.at[slot, side, pl.ds(0, tiles)],
                psend.at[slot, 1, side], precv.at[slot, 1, 1 - side], precv.at[slot, 1, side],
            ))
            for dx in (-1, 1):
                far = (dx + 1) // 2
                step.append(moved(
                    (dx, dy), PKP.at[side, 0 if dx < 0 else tiles - 1], RKC.at[slot, 1 - side, 1 - far],
                    RKC.at[slot, side, far],
                    psend.at[slot, 2 + side, far], precv.at[slot, 2 + 1 - side, 1 - far], precv.at[slot, 2 + side, far],
                ))
        go(step)
        if meanwhile is not None:
            meanwhile()
        land(step)

        def place(side, tile, m, i):
            if side == 0:
                turn = (8 - span - m * span) % 8
            else:
                turn = (-m * span) % 8
            tile = pltpu.roll(tile, turn, 0) if turn else tile
            field[i, rows(0 if side == 0 else 5), :] = tile

        for side, dy in ((0, -1), (1, 1)):
            _, _, there = neighbour(0, dy)

            @pl.when(there)
            def _():
                def body(g):
                    tile = RKP[slot, side, g]
                    for m in range(per):
                        place(side, tile, m, W + g * per + m)

                loop(0, tiles, body)

            for far, dx in ((0, -1), (1, 1)):
                _, _, there = neighbour(dx, dy)

                @pl.when(there)
                def _():
                    tile = RKC[slot, side, far]
                    for depth in range(width - 1):
                        if dx < 0:
                            place(side, tile, per - 1 - depth, W - 1 - depth)
                        else:
                            place(side, tile, depth, W + NX + depth)

    def restrict(field, i):
        x = i - W
        for j, _, res in residuals(field, i, tuple(range(1, TILES - 1))):
            t = j - 1
            for k in range(2):
                scaled = PR[k, x, 8 * t:8 * t + 8, :] * res
                for h in range(2):
                    both = jnp.concatenate(
                        [scaled[:, 256 * h:256 * h + 128], scaled[:, 256 * h + 128:256 * h + 256]], axis=0
                    )
                    high = both.astype(bf16)
                    at = pl.multiple_of((16 * k + x) * 128 + (t * 4 + 2 * h) * 8, 16)
                    WH[pl.ds(at, 16), :] = high
                    WL[pl.ds(at, 16), :] = (both - high.astype(f32)).astype(bf16)

    def wide(src, dst, parity, lists):
        out = []
        for n, (dx, dy) in enumerate(NEAR):
            if lists:
                def rect(ax, ay):
                    x0, x1 = max(-1, ax - 1) + 1, min(1, ax + 1) + 2
                    y0, y1 = max(-1, ay - 1) + 1, min(1, ay + 1) + 2
                    return pl.ds(x0, x1 - x0), pl.ds(y0, y1 - y0)
                give, take = rect(dx, dy), rect(-dx, -dy)
                piece, put, get = src.at[give], dst.at[(2 - dx, 2 - dy) + give], dst.at[(2 + dx, 2 + dy) + take]
            else:
                piece, put, get = src, dst.at[2 - dx, 2 - dy], dst.at[2 + dx, 2 + dy]
            outer = max(abs(dx), abs(dy)) == 2
            out.append(((10 * outer + 2 * abs(dy) + abs(dx)), moved(
                (dx, dy), piece, put, get, wsend.at[3 + parity, n], wrecv.at[3 + parity, 23 - n],
                wrecv.at[3 + parity, n],
            )))
        return [entry for _, entry in sorted(out, key=lambda pair: -pair[0])]

    def jacobi(table, near, far):
        every_row = [lambda r=r: table[r // 8, r % 8:r % 8 + 1, :] for r in range(72)]
        corner = [r for r in range(72) if r // 8 in (0, 2, 6, 8)]
        side = [r for r in range(72) if r // 8 not in (0, 2, 6, 8)]
        near()
        partly = []
        for m in range(8):
            at = cols_r[:, 128 * m:128 * m + 128]
            partly.append(pick_from(every_row, at, None, side))
        far()
        for m in range(8):
            at = cols_r[:, 128 * m:128 * m + 128]
            got = pick_from(every_row, at, partly[m], corner)
            coupled = jnp.sum(got * off_r[:, 128 * m:128 * m + 128], axis=0, keepdims=True)
            mine = table[4, m:m + 1, :]
            Y[m:m + 1, :] = mine + omega * (RATN[4, m:m + 1, :] - mine - coupled)

    def coarse(field, cycle):
        ones = jnp.ones((16, 128), bf16)
        along = (((1,), (1,)), ((), ()))
        sums = lax.dot_general(ones, WH[...], along, preferred_element_type=f32)
        sums = sums + lax.dot_general(ones, WL[...], along, preferred_element_type=f32)
        for r in range(3):
            if r < 2:
                part = HOT[8 * r:8 * r + 8, :] * sums[0:8]
            else:
                part = HOT[16:24, :] * sums[0:8]
            if r % 2 == 0:
                kept = part
            if r == 1:
                both = jnp.concatenate([kept, part], axis=0)
                high = both.astype(bf16)
                AB[0:16, :] = high
                AB[32:48, :] = (both - high.astype(f32)).astype(bf16)
            if r == 2:
                both = jnp.concatenate([part, jnp.zeros_like(part)], axis=0)
                high = both.astype(bf16)
                AB[16:32, :] = high
                AB[48:64, :] = (both - high.astype(f32)).astype(bf16)
        listed = jnp.dot(AB[...], LHOT[...], preferred_element_type=f32)
        listed = listed[0:32] + listed[32:64]
        for r in range(18):
            o, h = r // 2, r % 2
            OUT[o // 3, o % 3, h:h + 1, :] = listed[r:r + 1, :]
        step = wide(OUT, ARR, 0, True)
        go(step)
        ARR[2, 2] = OUT[...]
        if cycle == 0:
            land(tables)
        land(step)
        for p in range(9):
            total = jnp.zeros((8, 128), f32)
            for o in range(9):
                at = INVN[p, o]
                sx, sy = p // 3 + o // 3, p % 3 + o % 3
                other = 8 - o
                for h in range(2):
                    got = pick(ARR[sx, sy, other // 3, other % 3, h:h + 1, :], at)
                    total = total + jnp.where((at >> 7) == h, got, 0.0)
            ratio = total * DIAN[p]
            RATN[p] = ratio
            TAB[0, p] = omega * ratio
        jacobi(TAB.at[0], lambda: None, lambda: None)
        for s in range(1, CJ - 1):
            table = TAB.at[s % 2]
            step = around(lambda o: Y, table, csend.at[s % 2], crecv.at[s % 2])
            go(step)
            table[4] = Y[...]
            jacobi(table, lambda: land(step[4:]), lambda: land(step[:4]))
        step = wide(Y, T25, 1, False)
        go(step)
        T25[2, 2] = Y[...]
        land(step[16:])
        for o in range(9):
            BASE[o] = (1.0 - omega) * T25[1 + o // 3, 1 + o % 3] + omega * RATN[o]

        def last_rows(o, got, inside):
            ox, oy = o // 3, o % 3
            at = jnp.concatenate([ENT[o, h, 0:8, :] for h in range(2)], axis=0).astype(jnp.int32)
            chosen = [
                r for r in range(72)
                if (1 <= ox + r // 24 <= 3 and 1 <= oy + (r // 8) % 3 <= 3) == inside
            ]
            return pick_from(
                [lambda r=r: T25[ox + r // 24, oy + (r // 8) % 3, r % 8:r % 8 + 1, :] for r in range(72)],
                at, got, chosen,
            )

        for o in range(9):
            at = jnp.concatenate([ENT[o, h, 16:24, :] for h in range(2)], axis=0).astype(jnp.int32)
            LASTB[o] = pick_from([lambda r=r: BASE[o, r:r + 1, :] for r in range(8)], at)
            LASTG[o] = last_rows(o, None, True)
        land(step[:16])
        for o in range(9):
            got = LASTG[o] if o == 4 else last_rows(o, LASTG[o], False)
            for h in range(2):
                coupled = jnp.sum(got[8 * h:8 * h + 8] * ENT[o, h, 8:16, :], axis=0, keepdims=True)
                LIST[o, h:h + 1, :] = LASTB[o, 8 * h:8 * h + 1, :] - omega * coupled

        for r4 in range(4):
            VT[8 * r4:8 * r4 + 8, :] = pick_from(
                [lambda r=r: LIST[r // 2, r % 2:r % 2 + 1, :] for r in range(18)], SLOT[8 * r4:8 * r4 + 8, :]
            )
        VT[...] = VT[...].T

        def correct(x, blocks):
            for t in blocks:
                total = field[x + W, T + 8 * t:T + 8 * t + 8, :]
                for k in range(2):
                    which = jnp.full((8, 128), 16 * k, jnp.int32) + x
                    spread = []
                    for zb in range(4):
                        b0 = (t * 4 + zb) * 8
                        spread.append(
                            jnp.take_along_axis(VT[b0:b0 + 8, :], which, axis=1, mode="promise_in_bounds")
                        )
                    total = total + PR[k, x, 8 * t:8 * t + 8, :] * jnp.concatenate(spread, axis=1)
                field[x + W, T + 8 * t:T + 8 * t + 8, :] = total

        for lo in (0, NX - 2):
            correct(lo, range(4))
            correct(lo + 1, range(4))
        loop(2, NX - 2, lambda x: correct(x, (0, 3)))
        return lambda: loop(2, NX - 2, lambda x: correct(x, (1, 2)))

    VT[...] = jnp.zeros_like(VT)
    for cycle in range(CYCLES):
        field = (P0, P2)[cycle]
        if cycle == 0:
            sweep(1, sweep_b_first)
        else:
            exchange_pressure(field, 3, 1)
            sweep(2, functools.partial(sweep_a, field))
            sweep(1, functools.partial(sweep_b, field, field))
        loop(W, W + NX, functools.partial(restrict, field))
        rest = coarse(field, cycle)
        exchange_pressure(field, 2, 0, rest)
        sweep(1, functools.partial(sweep_a, field))
        sweep(0, functools.partial(sweep_b, field, P2))
    back = pltpu.make_async_copy(P2.at[center], out_h, in_sem.at[0])
    back.start()
    back.wait()


def shards(rhs, perm_h, perm_v, prolong, blk_slot, recv_slot, coarse_cols, coarse_off, coarse_diag):
    padded = pltpu.VMEM((2 * W + NX, 2 * T + NY, NZ), f32)
    hbm = pl.BlockSpec(memory_space=pltpu.HBM)
    i32 = jnp.int32
    return pl.pallas_call(
        kernel,
        out_shape=jax.ShapeDtypeStruct(rhs.shape, f32),
        in_specs=[hbm] * 9,
        out_specs=hbm,
        scratch_shapes=[padded] * 10
        + [
            pltpu.VMEM((2, NX, NY, NZ), f32),
            pltpu.VMEM((2, NX, 8, NZ), f32),
            pltpu.VMEM((2, NX + 4, 8, NZ), f32),
            pltpu.VMEM((2, 8, 8, NZ), f32),
            pltpu.VMEM((2, 2, 8, 8, NZ), f32),
            pltpu.VMEM((2, 2, 2, 8, NZ), f32),
            pltpu.VMEM((4096, 128), bf16),
            pltpu.VMEM((4096, 128), bf16),
            pltpu.VMEM((24, 4096), f32),
            pltpu.VMEM((4096, 128), bf16),
            pltpu.VMEM((64, 4096), bf16),
            pltpu.VMEM((32, 128), i32),
            pltpu.VMEM((128, 128), i32),
            pltpu.VMEM((128, 128), f32),
            pltpu.VMEM((24, 128), i32),
            pltpu.VMEM((9, 9, 8, 128), i32),
            pltpu.VMEM((9, 8, 128), f32),
            pltpu.VMEM((9, 2, 24, 128), f32),
            pltpu.VMEM((9, 2, 24, 128), f32),
            pltpu.VMEM((3, 3, 2, 128), f32),
            pltpu.VMEM((5, 5, 3, 3, 2, 128), f32),
            pltpu.VMEM((9, 8, 128), f32),
            pltpu.VMEM((2, 9, 8, 128), f32),
            pltpu.VMEM((5, 5, 8, 128), f32),
            pltpu.VMEM((9, 2, 128), f32),
            pltpu.VMEM((8, 128), f32),
            pltpu.VMEM((9, 8, 128), f32),
            pltpu.VMEM((9, 16, 128), f32),
            pltpu.VMEM((9, 16, 128), f32),
            pltpu.VMEM((2, NX, 128), i32),
            pltpu.VMEM((1, 2304), i32),
            pltpu.VMEM((8, 1024), i32),
            pltpu.VMEM((8, 1024), f32),
            pltpu.VMEM((1, 1024), f32),
            pltpu.SemaphoreType.DMA((9,)),
            pltpu.SemaphoreType.DMA((4, 6)),
            pltpu.SemaphoreType.DMA((4, 6)),
            pltpu.SemaphoreType.DMA((2, 4, 2)),
            pltpu.SemaphoreType.DMA((2, 4, 2)),
            pltpu.SemaphoreType.DMA((2, 9)),
            pltpu.SemaphoreType.DMA((2, 9)),
            pltpu.SemaphoreType.DMA((5, 24)),
            pltpu.SemaphoreType.DMA((5, 24)),
        ],
        compiler_params=pltpu.CompilerParams(
            collective_id=0, has_side_effects=True, vmem_limit_bytes=63 << 20
        ),
    )(rhs, perm_h, perm_v, prolong, blk_slot, recv_slot.T, coarse_cols, coarse_off, coarse_diag)


def solution(mesh):
    placed = (
        P("sx", "sy", None),
        P("sx", "sy", None),
        P("sx", "sy", None),
        P(None, "sx", "sy", None),
        P(None, "sx", "sy"),
        P(None, ("sx", "sy")),
        P(None, ("sx", "sy")),
        P(None, ("sx", "sy")),
        P(None, ("sx", "sy")),
    )
    return jax.shard_map(
        shards, mesh=mesh, in_specs=placed, out_specs=P("sx", "sy", None), check_vma=False
    )
```

```python
import functools

import jax
import jax.numpy as jnp
from jax import lax
from jax.experimental import pallas as pl
from jax.experimental.pallas import tpu as pltpu
from jax.sharding import PartitionSpec as P

CYCLES = 2
CJ = 4

storage_coef = 0.01
cheb_low = 0.25
cheb_high = 2.0
omega = 0.8

THETA = 0.5 * (cheb_high + cheb_low)
DELTA = 0.5 * (cheb_high - cheb_low)
SIGMA = THETA / DELTA
RHO0 = 1.0 / SIGMA
RHO1 = 1.0 / (2.0 * SIGMA - RHO0)
ALPHA = RHO1 * RHO0
BETA = 2.0 * RHO1 / DELTA

W = 3
T = 8
NX, NY, NZ = 16, 32, 512
TILES = (NY + 2 * T) // 8
MESH = pl.DeviceIdType.MESH
AROUND = (0, 2, 6, 8, 3, 5, 1, 7)
NEAR = tuple((dx, dy) for dx in range(-2, 3) for dy in range(-2, 3) if (dx, dy) != (0, 0))
f32 = jnp.float32
bf16 = jnp.bfloat16


def neighbour(dx, dy):
    x = lax.axis_index("sx") + dx
    y = lax.axis_index("sy") + dy
    there = (x >= 0) & (x < lax.axis_size("sx")) & (y >= 0) & (y < lax.axis_size("sy"))
    return x, y, there


def inverse(value):
    guess = pl.reciprocal(value, approx=True)
    return guess * (2.0 - value * guess)


def harmonic(left, right):
    total = left + right
    return 2.0 * left * right * inverse(jnp.where(total == 0.0, 1.0, total))


def pick(row, at):
    return jnp.take_along_axis(
        jnp.broadcast_to(row, at.shape), at & 127, axis=1, mode="promise_in_bounds"
    )


def pick_from(table_rows, at, got=None, chosen=None):
    high = at >> 7
    got = jnp.zeros(at.shape, f32) if got is None else got
    for r, row in enumerate(table_rows):
        if chosen is None or r in chosen:
            got = jnp.where(high == r, pick(row(), at), got)
    return got


def kernel(
    rhs_h, ph_h, pv_h, pr_h, slot_h, recv_h, cols_h, off_h, diag_h, out_h,
    RHS, PH, PV, TE, TN, TU, INV, P0, P1, P2, PR, PKS, PKC, RKS, PKP, RKP, RKC,
    WH, WL, HOT, LHOT, AB, SLOT, LT, VT, RIDX, INVN, DIAN, MSG, ENT,
    OUT, ARR, RATN, TAB, T25, LIST, Y, BASE, LASTB, LASTG,
    slot_r, recv_r, cols_r, off_r, diag_r,
    in_sem, fsend, frecv, psend, precv, csend, crecv, wsend, wrecv,
):
    sub = lax.broadcasted_iota(jnp.int32, (8, 128), 0)
    lane = lax.broadcasted_iota(jnp.int32, (8, 128), 1)
    sub512 = lax.broadcasted_iota(jnp.int32, (8, NZ), 0)
    lane512 = lax.broadcasted_iota(jnp.int32, (8, NZ), 1)

    def rows(j):
        return slice(8 * j, 8 * j + 8)

    inner = pl.ds(T, NY)
    center = (pl.ds(W, NX), inner, slice(None))
    loads = [
        pltpu.make_async_copy(src, dst, in_sem.at[n])
        for n, (src, dst) in enumerate(
            [(ph_h, PH.at[center]), (pv_h, PV.at[center]), (rhs_h, RHS.at[center]),
             (slot_h, slot_r), (recv_h, recv_r), (cols_h, cols_r), (off_h, off_r), (diag_h, diag_r),
             (pr_h, PR)]
        )
    ]
    for load in loads:
        load.start()

    bar = pltpu.get_barrier_semaphore()
    for o in AROUND:
        x, y, there = neighbour(o // 3 - 1, o % 3 - 1)

        @pl.when(there)
        def _():
            pl.semaphore_signal(bar, inc=1, device_id=(x, y), device_id_type=MESH)

    def loop(lo, hi, fn, per=2):
        steps = (hi - lo) // per

        def body(n, carry):
            for q in range(per):
                fn(lo + per * n + q)
            return carry

        lax.fori_loop(0, steps, body, 0)
        for i in range(lo + per * steps, hi):
            fn(i)

    def clear(view):
        def one(i):
            view[i] = jnp.zeros(view.shape[1:], f32)

        loop(0, view.shape[0], one)

    for array in (PH, PV, RHS, P0, P2):
        for dx, strip in ((-1, pl.ds(0, W)), (1, pl.ds(W + NX, W))):
            _, _, there = neighbour(dx, 0)

            @pl.when(jnp.logical_not(there))
            def _():
                clear(array.at[strip])

    for i in (0, 2 * W + NX - 1):
        for j in (0, TILES - 1):
            PH[i, rows(j), :] = jnp.zeros((8, NZ), f32)
    for side, dy in ((0, -1), (1, 1)):
        _, _, there = neighbour(0, dy)

        @pl.when(jnp.logical_not(there))
        def _():
            clear(RKS.at[side])
            clear(P0.at[:, pl.ds(0 if side == 0 else T + NY, T), :])
            clear(P2.at[:, pl.ds(0 if side == 0 else T + NY, T), :])

    for dx, strip in ((-1, pl.ds(0, 2)), (1, pl.ds(NX + 2, 2))):
        _, _, there = neighbour(dx, 0)

        @pl.when(jnp.logical_not(there))
        def _():
            clear(RKS.at[0, strip])
            clear(RKS.at[1, strip])

    for load in loads[:3]:
        load.wait()

    def pack_first(x):
        i = x + W
        a, b, c = PH[i, rows(1), :], PV[i, rows(1), :], RHS[i, rows(1), :]
        PKS[0, x] = jnp.where(sub512 < 3, a, jnp.where(sub512 < 5, pltpu.roll(b, 3, 0), pltpu.roll(c, 5, 0)))
        a, b, c = PH[i, rows(4), :], PV[i, rows(4), :], RHS[i, rows(4), :]
        PKS[1, x] = jnp.where(sub512 >= 5, a, jnp.where(sub512 >= 3, pltpu.roll(b, 5, 0), pltpu.roll(c, 3, 0)))

    loop(0, NX, pack_first)
    for far, near_x, next_x in ((0, 0, 1), (1, NX - 1, NX - 2)):
        PKC[0, far] = jnp.where(sub512 == 7, pltpu.roll(PKS[0, next_x], 7, 0), PKS[0, near_x])
        PKC[1, far] = jnp.where(sub512 == 0, pltpu.roll(PKS[1, next_x], 1, 0), PKS[1, near_x])

    peers = sum(neighbour(o // 3 - 1, o % 3 - 1)[2].astype(jnp.int32) for o in AROUND)
    pl.semaphore_wait(bar, peers)

    def go(copies):
        for there, copy, _ in copies:
            @pl.when(there)
            def _():
                copy.start()

    def land(copies):
        for there, copy, arrive in copies:
            @pl.when(there)
            def _():
                arrive.wait_recv()
                copy.wait_send()

    def moved(to, src, there_dst, here_dst, send, recv_there, recv_here):
        x, y, there = neighbour(*to)
        copy = pltpu.make_async_remote_copy(
            src, there_dst, send, recv_there, device_id=(x, y), device_id_type=MESH
        )
        arrive = pltpu.make_async_remote_copy(
            here_dst, here_dst, send, recv_here, device_id=(x, y), device_id_type=MESH
        )
        return there, copy, arrive

    def x_strips(field, src, base, width, send, recv):
        out = []
        for dx in (-1, 1):
            if dx < 0:
                take, put, get = base, W + NX, W - width
            else:
                take, put, get = base + NX - width, W - width, W + NX
            pick_y = inner if base else slice(None)
            out.append(moved(
                (dx, 0), src.at[pl.ds(take, width), pick_y, :], field.at[pl.ds(put, width), inner, :],
                field.at[pl.ds(get, width), inner, :],
                send.at[(dx + 1) // 2], recv.at[(1 - dx) // 2], recv.at[(dx + 1) // 2],
            ))
        return out

    first = []
    for dy in (-1, 1):
        side = (dy + 1) // 2
        for dx in (0, -1, 1):
            src = PKS.at[side] if dx == 0 else PKC.at[side, (dx + 1) // 2]
            put = {0: pl.ds(2, NX), -1: NX + 2, 1: 1}[dx]
            get = {0: pl.ds(2, NX), -1: 1, 1: NX + 2}[dx]
            first.append(moved(
                (dx, dy), src, RKS.at[1 - side, put], RKS.at[side, get],
                fsend.at[3, dx + 1 + 3 * side], frecv.at[3, 1 - dx + 3 * (1 - side)],
                frecv.at[3, dx + 1 + 3 * side],
            ))
    for n, (field, src, width) in enumerate(((PH, ph_h, 3), (PV, pv_h, 2), (RHS, rhs_h, 2))):
        first += x_strips(field, src, 0, width, fsend.at[n], frecv.at[n])
    go(first)

    for load in loads[3:]:
        load.wait()
    for k in range(2):
        for x8 in range(2):
            raw = slot_r[k, 8 * x8:8 * x8 + 8, :]
            order = (((lane >> 5) << 3) + (lane & 7)) * 4 + ((lane >> 3) & 3)
            SLOT[pl.ds(16 * k + 8 * x8, 8), :] = jnp.take_along_axis(
                raw, order, axis=1, mode="promise_in_bounds"
            )
    RIDX[...] = jnp.full_like(RIDX, 1024)
    for r in range(18):
        RIDX[r:r + 1, :] = recv_r[0:1, r * 128:(r + 1) * 128]
    low = lax.broadcasted_iota(jnp.int32, (128, 128), 0)
    cnum = lane.astype(f32) + 1.0
    for o in range(9):
        total = jnp.zeros((8, 128), f32)
        for h in range(2):
            ids = RIDX[2 * o + h:2 * o + h + 1, :]
            a = jnp.where(jnp.broadcast_to(ids >> 7, (8, 128)) == sub, cnum + 128.0 * h, 0.0)
            b = (jnp.broadcast_to(ids & 127, (128, 128)) == low).astype(f32)
            total = total + lax.dot_general(
                a.astype(bf16), b.astype(bf16), (((1,), (1,)), ((), ())),
                preferred_element_type=f32,
            )
        INVN[4, o] = (total + 0.5).astype(jnp.int32) - 1
    for m in range(8):
        DIAN[4, m:m + 1, :] = diag_r[0:1, m * 128:(m + 1) * 128]
    DIAN[4] = 1.0 / DIAN[4]
    for o in range(9):
        for h in range(2):
            at = jnp.broadcast_to(RIDX[2 * o + h:2 * o + h + 1, :], (8, 128))
            at = jnp.where(at == 1024, 0, at)
            cols = jnp.zeros((8, 128), f32)
            offs = jnp.zeros((8, 128), f32)
            for m in range(8):
                piece = slice(128 * m, 128 * m + 128)
                hit = (at >> 7) == m
                cols = jnp.where(hit, pick(cols_r[:, piece].astype(f32), at), cols)
                offs = jnp.where(hit, pick(off_r[:, piece], at), offs)
            MSG[o, h, 0:8, :] = cols
            MSG[o, h, 8:16, :] = offs
            MSG[o, h, 16:24, :] = at.astype(f32)
    ENT[4] = MSG[4]

    def around(src, dst, send, recv):
        out = []
        for o in AROUND:
            out.append(moved(
                (o // 3 - 1, o % 3 - 1), src(o), dst.at[8 - o], dst.at[o],
                send.at[o], recv.at[8 - o], recv.at[o],
            ))
        return out

    tables = []
    for o in AROUND:
        to = (o // 3 - 1, o % 3 - 1)
        tables.append(moved(to, INVN.at[4], INVN.at[8 - o], INVN.at[o], wsend.at[0, o], wrecv.at[0, 8 - o], wrecv.at[0, o]))
        tables.append(moved(to, DIAN.at[4], DIAN.at[8 - o], DIAN.at[o], wsend.at[1, o], wrecv.at[1, 8 - o], wrecv.at[1, o]))
    tables += around(lambda o: MSG.at[o], ENT, wsend.at[2], wrecv.at[2])

    LT[...] = jnp.zeros_like(LT)
    LT[0:32, :] = SLOT[...] & 127
    LT[...] = LT[...].T
    lane_all = lax.broadcasted_iota(jnp.int32, (128, 128), 1)
    row24 = lax.broadcasted_iota(jnp.int32, (24, 128), 0)
    for kx in range(32):
        line = jnp.broadcast_to(SLOT[kx:kx + 1, :] >> 7, (24, 128))
        HOT[:, kx * 128:(kx + 1) * 128] = (line == row24).astype(f32)
        LHOT[kx * 128:(kx + 1) * 128, :] = (
            jnp.broadcast_to(LT[:, kx:kx + 1], (128, 128)) == lane_all
        ).astype(f32).astype(bf16)
    AB[...] = jnp.zeros_like(AB)

    def edge_x(i, tiles):
        for j in tiles:
            TE[i, rows(j), :] = harmonic(PH[i, rows(j), :], PH[i + 1, rows(j), :])

    def edge_yz(i, new, done):
        for j in new:
            ctr = PH[i, rows(j), :]
            if j < TILES - 1:
                up = PH[i, 8 * j + 1:8 * j + 9, :]
            else:
                up = pltpu.roll(ctr, 7, 0)
            TN[i, rows(j), :] = harmonic(ctr, up)
            pv = PV[i, rows(j), :]
            TU[i, rows(j), :] = jnp.where(
                lane512 == NZ - 1, 0.0, harmonic(pv, pltpu.roll(pv, NZ - 1, 1))
            )
        for j in done:
            tn = TN[i, rows(j), :]
            down = TN[i, 8 * j - 1:8 * j + 7, :] if j > 0 else pltpu.roll(tn, 1, 0)
            tu = TU[i, rows(j), :]
            total = storage_coef + TE[i, rows(j), :] + TE[i - 1, rows(j), :] + tn + down + tu + pltpu.roll(tu, 1, 1)
            inv = inverse(total)
            INV[i, rows(j), :] = inv
            P1[i, rows(j), :] = (1.0 / THETA) * inv * RHS[i, rows(j), :]

    every = tuple(range(TILES))
    loop(W, W + NX - 1, lambda i: edge_x(i, (1, 2, 3, 4)))
    loop(W + 1, W + NX - 1, lambda i: edge_yz(i, (1, 2, 3), (2, 3)))

    land(first)
    go(tables)
    for near_x, next_x in ((1, 0), (NX + 2, NX + 3)):
        RKS[0, next_x] = pltpu.roll(RKS[0, near_x], 7, 0)
        RKS[1, next_x] = pltpu.roll(RKS[1, near_x], 1, 0)

    def unpack_first(i):
        got = RKS[0, i - 1]
        PH[i, rows(0), :] = jnp.where(sub512 >= 5, got, 0.0)
        PV[i, rows(0), :] = jnp.where(sub512 >= 6, pltpu.roll(got, 3, 0), 0.0)
        RHS[i, rows(0), :] = jnp.where(sub512 >= 6, pltpu.roll(got, 5, 0), 0.0)
        got = RKS[1, i - 1]
        PH[i, rows(5), :] = jnp.where(sub512 < 3, got, 0.0)
        PV[i, rows(5), :] = jnp.where(sub512 < 2, pltpu.roll(got, 5, 0), 0.0)
        RHS[i, rows(5), :] = jnp.where(sub512 < 2, pltpu.roll(got, 3, 0), 0.0)

    loop(1, NX + 5, unpack_first)
    for lo, hi in ((0, W), (W + NX - 1, 2 * W + NX - 1)):
        loop(lo, hi, lambda i: edge_x(i, every))
    loop(W, W + NX - 1, lambda i: edge_x(i, (0, 5)))
    for lo, hi in ((1, W + 1), (W + NX - 1, 2 * W + NX - 1)):
        loop(lo, hi, lambda i: edge_yz(i, every, every))
    loop(W + 1, W + NX - 1, lambda i: edge_yz(i, (0, 4, 5), (0, 1, 4, 5)))

    def residuals(field, i, tiles):
        before = None
        for j in tiles:
            ctr = field[i, rows(j), :]
            acc = RHS[i, rows(j), :] - storage_coef * ctr
            acc = acc + TE[i, rows(j), :] * (field[i + 1, rows(j), :] - ctr)
            acc = acc + TE[i - 1, rows(j), :] * (field[i - 1, rows(j), :] - ctr)
            fz = TU[i, rows(j), :] * (pltpu.roll(ctr, NZ - 1, 1) - ctr)
            acc = acc + fz - pltpu.roll(fz, 1, 1)
            up = pltpu.roll(ctr, 7, 0)
            if j < TILES - 1:
                up = jnp.where(sub512 == 7, pltpu.roll(field[i, rows(j + 1), :], 7, 0), up)
            fn = TN[i, rows(j), :] * (up - ctr)
            turned = pltpu.roll(fn, 1, 0)
            if before is not None:
                fs = jnp.where(sub512 == 0, before, turned)
            elif j > 0:
                fs = TN[i, 8 * j - 1:8 * j + 7, :] * (ctr - field[i, 8 * j - 1:8 * j + 7, :])
            else:
                fs = turned
            before = turned
            yield j, ctr, acc + fn - fs

    def sweep(extent, update):
        tiles = tuple(range(TILES)) if extent > 0 else tuple(range(1, TILES - 1))
        loop(W - extent, W + NX + extent, lambda i: update(i, tiles))

    def sweep_a(field, i, tiles):
        for j, ctr, res in residuals(field, i, tiles):
            P1[i, rows(j), :] = ctr + (1.0 / THETA) * INV[i, rows(j), :] * res

    def sweep_b_first(i, tiles):
        for j, ctr, res in residuals(P1, i, tiles):
            P0[i, rows(j), :] = (1.0 + ALPHA) * ctr + BETA * INV[i, rows(j), :] * res

    def sweep_b(old, new, i, tiles):
        for j, ctr, res in residuals(P1, i, tiles):
            new[i, rows(j), :] = (1.0 + ALPHA) * ctr - ALPHA * old[i, rows(j), :] + BETA * INV[i, rows(j), :] * res

    def exchange_pressure(field, width, slot, meanwhile=None):
        per = 8 // (2 if width == 2 else 4)
        span = 8 // per
        tiles = NX // per

        def pack(g):
            a = b = None
            for m in range(per):
                i = W + g * per + m
                one = field[i, rows(1), :]
                two = field[i, rows(4), :]
                one = one if m == 0 else pltpu.roll(one, m * span, 0)
                two = two if (m + 1) * span == 8 else pltpu.roll(two, (m + 1) * span, 0)
                a = one if a is None else jnp.where(sub512 >= m * span, one, a)
                b = two if b is None else jnp.where(sub512 >= m * span, two, b)
            PKP[0, g] = a
            PKP[1, g] = b

        loop(0, tiles, pack)
        step = x_strips(field, field, W, width, psend.at[slot, 0], precv.at[slot, 0])
        for dy in (-1, 1):
            side = (dy + 1) // 2
            step.append(moved(
                (0, dy), PKP.at[side, pl.ds(0, tiles)], RKP.at[slot, 1 - side, pl.ds(0, tiles)],
                RKP.at[slot, side, pl.ds(0, tiles)],
                psend.at[slot, 1, side], precv.at[slot, 1, 1 - side], precv.at[slot, 1, side],
            ))
            for dx in (-1, 1):
                far = (dx + 1) // 2
                step.append(moved(
                    (dx, dy), PKP.at[side, 0 if dx < 0 else tiles - 1], RKC.at[slot, 1 - side, 1 - far],
                    RKC.at[slot, side, far],
                    psend.at[slot, 2 + side, far], precv.at[slot, 2 + 1 - side, 1 - far], precv.at[slot, 2 + side, far],
                ))
        go(step)
        if meanwhile is not None:
            meanwhile()
        land(step)

        def place(side, tile, m, i):
            if side == 0:
                turn = (8 - span - m * span) % 8
            else:
                turn = (-m * span) % 8
            tile = pltpu.roll(tile, turn, 0) if turn else tile
            field[i, rows(0 if side == 0 else 5), :] = tile

        for side, dy in ((0, -1), (1, 1)):
            _, _, there = neighbour(0, dy)

            @pl.when(there)
            def _():
                def body(g):
                    tile = RKP[slot, side, g]
                    for m in range(per):
                        place(side, tile, m, W + g * per + m)

                loop(0, tiles, body)

            for far, dx in ((0, -1), (1, 1)):
                _, _, there = neighbour(dx, dy)

                @pl.when(there)
                def _():
                    tile = RKC[slot, side, far]
                    for depth in range(width - 1):
                        if dx < 0:
                            place(side, tile, per - 1 - depth, W - 1 - depth)
                        else:
                            place(side, tile, depth, W + NX + depth)

    def restrict(field, i):
        x = i - W
        for j, _, res in residuals(field, i, tuple(range(1, TILES - 1))):
            t = j - 1
            for k in range(2):
                scaled = PR[k, x, 8 * t:8 * t + 8, :] * res
                for h in range(2):
                    both = jnp.concatenate(
                        [scaled[:, 256 * h:256 * h + 128], scaled[:, 256 * h + 128:256 * h + 256]], axis=0
                    )
                    high = both.astype(bf16)
                    at = pl.multiple_of((16 * k + x) * 128 + (t * 4 + 2 * h) * 8, 16)
                    WH[pl.ds(at, 16), :] = high
                    WL[pl.ds(at, 16), :] = (both - high.astype(f32)).astype(bf16)

    def wide(src, dst, parity, lists):
        out = []
        for n, (dx, dy) in enumerate(NEAR):
            if lists:
                def rect(ax, ay):
                    x0, x1 = max(-1, ax - 1) + 1, min(1, ax + 1) + 2
                    y0, y1 = max(-1, ay - 1) + 1, min(1, ay + 1) + 2
                    return pl.ds(x0, x1 - x0), pl.ds(y0, y1 - y0)
                give, take = rect(dx, dy), rect(-dx, -dy)
                piece, put, get = src.at[give], dst.at[(2 - dx, 2 - dy) + give], dst.at[(2 + dx, 2 + dy) + take]
            else:
                piece, put, get = src, dst.at[2 - dx, 2 - dy], dst.at[2 + dx, 2 + dy]
            outer = max(abs(dx), abs(dy)) == 2
            out.append(((10 * outer + 2 * abs(dy) + abs(dx)), moved(
                (dx, dy), piece, put, get, wsend.at[3 + parity, n], wrecv.at[3 + parity, 23 - n],
                wrecv.at[3 + parity, n],
            )))
        return [entry for _, entry in sorted(out, key=lambda pair: -pair[0])]

    def jacobi(table, near, far):
        every_row = [lambda r=r: table[r // 8, r % 8:r % 8 + 1, :] for r in range(72)]
        corner = [r for r in range(72) if r // 8 in (0, 2, 6, 8)]
        side = [r for r in range(72) if r // 8 not in (0, 2, 6, 8)]
        near()
        partly = []
        for m in range(8):
            at = cols_r[:, 128 * m:128 * m + 128]
            partly.append(pick_from(every_row, at, None, side))
        far()
        for m in range(8):
            at = cols_r[:, 128 * m:128 * m + 128]
            got = pick_from(every_row, at, partly[m], corner)
            coupled = jnp.sum(got * off_r[:, 128 * m:128 * m + 128], axis=0, keepdims=True)
            mine = table[4, m:m + 1, :]
            Y[m:m + 1, :] = mine + omega * (RATN[4, m:m + 1, :] - mine - coupled)

    def coarse(field, cycle):
        ones = jnp.ones((16, 128), bf16)
        along = (((1,), (1,)), ((), ()))
        sums = lax.dot_general(ones, WH[...], along, preferred_element_type=f32)
        sums = sums + lax.dot_general(ones, WL[...], along, preferred_element_type=f32)
        for r in range(3):
            if r < 2:
                part = HOT[8 * r:8 * r + 8, :] * sums[0:8]
            else:
                part = HOT[16:24, :] * sums[0:8]
            if r % 2 == 0:
                kept = part
            if r == 1:
                both = jnp.concatenate([kept, part], axis=0)
                high = both.astype(bf16)
                AB[0:16, :] = high
                AB[32:48, :] = (both - high.astype(f32)).astype(bf16)
            if r == 2:
                both = jnp.concatenate([part, jnp.zeros_like(part)], axis=0)
                high = both.astype(bf16)
                AB[16:32, :] = high
                AB[48:64, :] = (both - high.astype(f32)).astype(bf16)
        listed = jnp.dot(AB[...], LHOT[...], preferred_element_type=f32)
        listed = listed[0:32] + listed[32:64]
        for r in range(18):
            o, h = r // 2, r % 2
            OUT[o // 3, o % 3, h:h + 1, :] = listed[r:r + 1, :]
        step = wide(OUT, ARR, 0, True)
        go(step)
        ARR[2, 2] = OUT[...]
        if cycle == 0:
            land(tables)
        land(step)
        for p in range(9):
            total = jnp.zeros((8, 128), f32)
            for o in range(9):
                at = INVN[p, o]
                sx, sy = p // 3 + o // 3, p % 3 + o % 3
                other = 8 - o
                for h in range(2):
                    got = pick(ARR[sx, sy, other // 3, other % 3, h:h + 1, :], at)
                    total = total + jnp.where((at >> 7) == h, got, 0.0)
            ratio = total * DIAN[p]
            RATN[p] = ratio
            TAB[0, p] = omega * ratio
        jacobi(TAB.at[0], lambda: None, lambda: None)
        for s in range(1, CJ - 1):
            table = TAB.at[s % 2]
            step = around(lambda o: Y, table, csend.at[s % 2], crecv.at[s % 2])
            go(step)
            table[4] = Y[...]
            jacobi(table, lambda: land(step[4:]), lambda: land(step[:4]))
        step = wide(Y, T25, 1, False)
        go(step)
        T25[2, 2] = Y[...]
        land(step[16:])
        for o in range(9):
            BASE[o] = (1.0 - omega) * T25[1 + o // 3, 1 + o % 3] + omega * RATN[o]

        def last_rows(o, got, inside):
            ox, oy = o // 3, o % 3
            at = jnp.concatenate([ENT[o, h, 0:8, :] for h in range(2)], axis=0).astype(jnp.int32)
            chosen = [
                r for r in range(72)
                if (1 <= ox + r // 24 <= 3 and 1 <= oy + (r // 8) % 3 <= 3) == inside
            ]
            return pick_from(
                [lambda r=r: T25[ox + r // 24, oy + (r // 8) % 3, r % 8:r % 8 + 1, :] for r in range(72)],
                at, got, chosen,
            )

        for o in range(9):
            at = jnp.concatenate([ENT[o, h, 16:24, :] for h in range(2)], axis=0).astype(jnp.int32)
            LASTB[o] = pick_from([lambda r=r: BASE[o, r:r + 1, :] for r in range(8)], at)
            LASTG[o] = last_rows(o, None, True)
        land(step[:16])
        for o in range(9):
            got = LASTG[o] if o == 4 else last_rows(o, LASTG[o], False)
            for h in range(2):
                coupled = jnp.sum(got[8 * h:8 * h + 8] * ENT[o, h, 8:16, :], axis=0, keepdims=True)
                LIST[o, h:h + 1, :] = LASTB[o, 8 * h:8 * h + 1, :] - omega * coupled

        for r4 in range(4):
            VT[8 * r4:8 * r4 + 8, :] = pick_from(
                [lambda r=r: LIST[r // 2, r % 2:r % 2 + 1, :] for r in range(18)], SLOT[8 * r4:8 * r4 + 8, :]
            )
        VT[...] = VT[...].T

        def correct(x, blocks):
            for t in blocks:
                total = field[x + W, T + 8 * t:T + 8 * t + 8, :]
                for k in range(2):
                    which = jnp.full((8, 128), 16 * k, jnp.int32) + x
                    spread = []
                    for zb in range(4):
                        b0 = (t * 4 + zb) * 8
                        spread.append(
                            jnp.take_along_axis(VT[b0:b0 + 8, :], which, axis=1, mode="promise_in_bounds")
                        )
                    total = total + PR[k, x, 8 * t:8 * t + 8, :] * jnp.concatenate(spread, axis=1)
                field[x + W, T + 8 * t:T + 8 * t + 8, :] = total

        for lo in (0, NX - 2):
            correct(lo, range(4))
            correct(lo + 1, range(4))
        loop(2, NX - 2, lambda x: correct(x, (0, 3)), 4)
        return lambda: loop(2, NX - 2, lambda x: correct(x, (1, 2)), 4)

    VT[...] = jnp.zeros_like(VT)
    for cycle in range(CYCLES):
        field = (P0, P2)[cycle]
        if cycle == 0:
            sweep(1, sweep_b_first)
        else:
            exchange_pressure(field, 3, 1)
            sweep(2, functools.partial(sweep_a, field))
            sweep(1, functools.partial(sweep_b, field, field))
        loop(W, W + NX, functools.partial(restrict, field))
        rest = coarse(field, cycle)
        exchange_pressure(field, 2, 0, rest)
        sweep(1, functools.partial(sweep_a, field))
        sweep(0, functools.partial(sweep_b, field, P2))
    back = pltpu.make_async_copy(P2.at[center], out_h, in_sem.at[0])
    back.start()
    back.wait()


def shards(rhs, perm_h, perm_v, prolong, blk_slot, recv_slot, coarse_cols, coarse_off, coarse_diag):
    padded = pltpu.VMEM((2 * W + NX, 2 * T + NY, NZ), f32)
    hbm = pl.BlockSpec(memory_space=pltpu.HBM)
    i32 = jnp.int32
    return pl.pallas_call(
        kernel,
        out_shape=jax.ShapeDtypeStruct(rhs.shape, f32),
        in_specs=[hbm] * 9,
        out_specs=hbm,
        scratch_shapes=[padded] * 10
        + [
            pltpu.VMEM((2, NX, NY, NZ), f32),
            pltpu.VMEM((2, NX, 8, NZ), f32),
            pltpu.VMEM((2, 2, 8, NZ), f32),
            pltpu.VMEM((2, NX + 4, 8, NZ), f32),
            pltpu.VMEM((2, 8, 8, NZ), f32),
            pltpu.VMEM((2, 2, 8, 8, NZ), f32),
            pltpu.VMEM((2, 2, 2, 8, NZ), f32),
            pltpu.VMEM((4096, 128), bf16),
            pltpu.VMEM((4096, 128), bf16),
            pltpu.VMEM((24, 4096), f32),
            pltpu.VMEM((4096, 128), bf16),
            pltpu.VMEM((64, 4096), bf16),
            pltpu.VMEM((32, 128), i32),
            pltpu.VMEM((128, 128), i32),
            pltpu.VMEM((128, 128), f32),
            pltpu.VMEM((24, 128), i32),
            pltpu.VMEM((9, 9, 8, 128), i32),
            pltpu.VMEM((9, 8, 128), f32),
            pltpu.VMEM((9, 2, 24, 128), f32),
            pltpu.VMEM((9, 2, 24, 128), f32),
            pltpu.VMEM((3, 3, 2, 128), f32),
            pltpu.VMEM((5, 5, 3, 3, 2, 128), f32),
            pltpu.VMEM((9, 8, 128), f32),
            pltpu.VMEM((2, 9, 8, 128), f32),
            pltpu.VMEM((5, 5, 8, 128), f32),
            pltpu.VMEM((9, 2, 128), f32),
            pltpu.VMEM((8, 128), f32),
            pltpu.VMEM((9, 8, 128), f32),
            pltpu.VMEM((9, 16, 128), f32),
            pltpu.VMEM((9, 16, 128), f32),
            pltpu.VMEM((2, NX, 128), i32),
            pltpu.VMEM((1, 2304), i32),
            pltpu.VMEM((8, 1024), i32),
            pltpu.VMEM((8, 1024), f32),
            pltpu.VMEM((1, 1024), f32),
            pltpu.SemaphoreType.DMA((9,)),
            pltpu.SemaphoreType.DMA((4, 6)),
            pltpu.SemaphoreType.DMA((4, 6)),
            pltpu.SemaphoreType.DMA((2, 4, 2)),
            pltpu.SemaphoreType.DMA((2, 4, 2)),
            pltpu.SemaphoreType.DMA((2, 9)),
            pltpu.SemaphoreType.DMA((2, 9)),
            pltpu.SemaphoreType.DMA((5, 24)),
            pltpu.SemaphoreType.DMA((5, 24)),
        ],
        compiler_params=pltpu.CompilerParams(
            collective_id=0, has_side_effects=True, vmem_limit_bytes=63 << 20
        ),
    )(rhs, perm_h, perm_v, prolong, blk_slot, recv_slot.T, coarse_cols, coarse_off, coarse_diag)


def solution(mesh):
    placed = (
        P("sx", "sy", None),
        P("sx", "sy", None),
        P("sx", "sy", None),
        P(None, "sx", "sy", None),
        P(None, "sx", "sy"),
        P(None, ("sx", "sy")),
        P(None, ("sx", "sy")),
        P(None, ("sx", "sy")),
        P(None, ("sx", "sy")),
    )
    return jax.shard_map(
        shards, mesh=mesh, in_specs=placed, out_specs=P("sx", "sy", None), check_vma=False
    )
```

```python
import functools

import jax
import jax.numpy as jnp
from jax import lax
from jax.experimental import pallas as pl
from jax.experimental.pallas import tpu as pltpu
from jax.sharding import PartitionSpec as P

CYCLES = 2
CJ = 4

storage_coef = 0.01
cheb_low = 0.25
cheb_high = 2.0
omega = 0.8

THETA = 0.5 * (cheb_high + cheb_low)
DELTA = 0.5 * (cheb_high - cheb_low)
SIGMA = THETA / DELTA
RHO0 = 1.0 / SIGMA
RHO1 = 1.0 / (2.0 * SIGMA - RHO0)
ALPHA = RHO1 * RHO0
BETA = 2.0 * RHO1 / DELTA

W = 3
T = 8
NX, NY, NZ = 16, 32, 512
TILES = (NY + 2 * T) // 8
MESH = pl.DeviceIdType.MESH
AROUND = (0, 2, 6, 8, 3, 5, 1, 7)
NEAR = tuple((dx, dy) for dx in range(-2, 3) for dy in range(-2, 3) if (dx, dy) != (0, 0))
f32 = jnp.float32
bf16 = jnp.bfloat16


def neighbour(dx, dy):
    x = lax.axis_index("sx") + dx
    y = lax.axis_index("sy") + dy
    there = (x >= 0) & (x < lax.axis_size("sx")) & (y >= 0) & (y < lax.axis_size("sy"))
    return x, y, there


def inverse(value):
    guess = pl.reciprocal(value, approx=True)
    return guess * (2.0 - value * guess)


def harmonic(left, right):
    total = left + right
    return 2.0 * left * right * inverse(jnp.where(total == 0.0, 1.0, total))


def pick(row, at):
    return jnp.take_along_axis(
        jnp.broadcast_to(row, at.shape), at & 127, axis=1, mode="promise_in_bounds"
    )


def pick_from(table_rows, at, got=None, chosen=None):
    high = at >> 7
    got = jnp.zeros(at.shape, f32) if got is None else got
    for r, row in enumerate(table_rows):
        if chosen is None or r in chosen:
            got = jnp.where(high == r, pick(row(), at), got)
    return got


def kernel(
    rhs_h, ph_h, pv_h, pr_h, slot_h, recv_h, cols_h, off_h, diag_h, out_h,
    RHS, PH, PV, TE, TN, TU, INV, P0, P1, P2, PR, PKS, PKC, RKS, PKP, RKP, RKC,
    WH, WL, HOT, LHOT, AB, SLOT, LT, VT, RIDX, INVN, DIAN, MSG, ENT,
    OUT, ARR, RATN, TAB, T25, LIST, Y, BASE, LASTB, LASTG,
    slot_r, recv_r, cols_r, off_r, diag_r,
    in_sem, fsend, frecv, psend, precv, csend, crecv, wsend, wrecv,
):
    sub = lax.broadcasted_iota(jnp.int32, (8, 128), 0)
    lane = lax.broadcasted_iota(jnp.int32, (8, 128), 1)
    sub512 = lax.broadcasted_iota(jnp.int32, (8, NZ), 0)
    lane512 = lax.broadcasted_iota(jnp.int32, (8, NZ), 1)

    def rows(j):
        return slice(8 * j, 8 * j + 8)

    inner = pl.ds(T, NY)
    center = (pl.ds(W, NX), inner, slice(None))
    loads = [
        pltpu.make_async_copy(src, dst, in_sem.at[n])
        for n, (src, dst) in enumerate(
            [(ph_h, PH.at[center]), (pv_h, PV.at[center]), (rhs_h, RHS.at[center]),
             (slot_h, slot_r), (recv_h, recv_r), (cols_h, cols_r), (off_h, off_r), (diag_h, diag_r),
             (pr_h, PR)]
        )
    ]
    for load in loads:
        load.start()

    bar = pltpu.get_barrier_semaphore()
    for o in AROUND:
        x, y, there = neighbour(o // 3 - 1, o % 3 - 1)

        @pl.when(there)
        def _():
            pl.semaphore_signal(bar, inc=1, device_id=(x, y), device_id_type=MESH)

    def loop(lo, hi, fn, per=2):
        steps = (hi - lo) // per

        def body(n, carry):
            for q in range(per):
                fn(lo + per * n + q)
            return carry

        lax.fori_loop(0, steps, body, 0)
        for i in range(lo + per * steps, hi):
            fn(i)

    def clear(view):
        def one(i):
            view[i] = jnp.zeros(view.shape[1:], f32)

        loop(0, view.shape[0], one)

    for array in (PH, PV, RHS, P0, P2):
        for dx, strip in ((-1, pl.ds(0, W)), (1, pl.ds(W + NX, W))):
            _, _, there = neighbour(dx, 0)

            @pl.when(jnp.logical_not(there))
            def _():
                clear(array.at[strip])

    for i in (0, 2 * W + NX - 1):
        for j in (0, TILES - 1):
            PH[i, rows(j), :] = jnp.zeros((8, NZ), f32)
    for side, dy in ((0, -1), (1, 1)):
        _, _, there = neighbour(0, dy)

        @pl.when(jnp.logical_not(there))
        def _():
            clear(RKS.at[side])
            clear(P0.at[:, pl.ds(0 if side == 0 else T + NY, T), :])
            clear(P2.at[:, pl.ds(0 if side == 0 else T + NY, T), :])

    for dx, strip in ((-1, pl.ds(0, 2)), (1, pl.ds(NX + 2, 2))):
        _, _, there = neighbour(dx, 0)

        @pl.when(jnp.logical_not(there))
        def _():
            clear(RKS.at[0, strip])
            clear(RKS.at[1, strip])

    for load in loads[:3]:
        load.wait()

    def pack_first(x):
        i = x + W
        a, b, c = PH[i, rows(1), :], PV[i, rows(1), :], RHS[i, rows(1), :]
        PKS[0, x] = jnp.where(sub512 < 3, a, jnp.where(sub512 < 5, pltpu.roll(b, 3, 0), pltpu.roll(c, 5, 0)))
        a, b, c = PH[i, rows(4), :], PV[i, rows(4), :], RHS[i, rows(4), :]
        PKS[1, x] = jnp.where(sub512 >= 5, a, jnp.where(sub512 >= 3, pltpu.roll(b, 5, 0), pltpu.roll(c, 3, 0)))

    loop(0, NX, pack_first)
    for far, near_x, next_x in ((0, 0, 1), (1, NX - 1, NX - 2)):
        PKC[0, far] = jnp.where(sub512 == 7, pltpu.roll(PKS[0, next_x], 7, 0), PKS[0, near_x])
        PKC[1, far] = jnp.where(sub512 == 0, pltpu.roll(PKS[1, next_x], 1, 0), PKS[1, near_x])

    peers = sum(neighbour(o // 3 - 1, o % 3 - 1)[2].astype(jnp.int32) for o in AROUND)
    pl.semaphore_wait(bar, peers)

    def go(copies):
        for there, copy, _ in copies:
            @pl.when(there)
            def _():
                copy.start()

    def land(copies):
        for there, copy, arrive in copies:
            @pl.when(there)
            def _():
                arrive.wait_recv()
                copy.wait_send()

    def moved(to, src, there_dst, here_dst, send, recv_there, recv_here):
        x, y, there = neighbour(*to)
        copy = pltpu.make_async_remote_copy(
            src, there_dst, send, recv_there, device_id=(x, y), device_id_type=MESH
        )
        arrive = pltpu.make_async_remote_copy(
            here_dst, here_dst, send, recv_here, device_id=(x, y), device_id_type=MESH
        )
        return there, copy, arrive

    def x_strips(field, src, base, width, send, recv):
        out = []
        for dx in (-1, 1):
            if dx < 0:
                take, put, get = base, W + NX, W - width
            else:
                take, put, get = base + NX - width, W - width, W + NX
            pick_y = inner if base else slice(None)
            out.append(moved(
                (dx, 0), src.at[pl.ds(take, width), pick_y, :], field.at[pl.ds(put, width), inner, :],
                field.at[pl.ds(get, width), inner, :],
                send.at[(dx + 1) // 2], recv.at[(1 - dx) // 2], recv.at[(dx + 1) // 2],
            ))
        return out

    first = []
    for dy in (-1, 1):
        side = (dy + 1) // 2
        for dx in (0, -1, 1):
            src = PKS.at[side] if dx == 0 else PKC.at[side, (dx + 1) // 2]
            put = {0: pl.ds(2, NX), -1: NX + 2, 1: 1}[dx]
            get = {0: pl.ds(2, NX), -1: 1, 1: NX + 2}[dx]
            first.append(moved(
                (dx, dy), src, RKS.at[1 - side, put], RKS.at[side, get],
                fsend.at[3, dx + 1 + 3 * side], frecv.at[3, 1 - dx + 3 * (1 - side)],
                frecv.at[3, dx + 1 + 3 * side],
            ))
    for n, (field, src, width) in enumerate(((PH, ph_h, 3), (PV, pv_h, 2), (RHS, rhs_h, 2))):
        first += x_strips(field, src, 0, width, fsend.at[n], frecv.at[n])
    go(first)

    for load in loads[3:]:
        load.wait()
    for k in range(2):
        for x8 in range(2):
            raw = slot_r[k, 8 * x8:8 * x8 + 8, :]
            order = (((lane >> 5) << 3) + (lane & 7)) * 4 + ((lane >> 3) & 3)
            SLOT[pl.ds(16 * k + 8 * x8, 8), :] = jnp.take_along_axis(
                raw, order, axis=1, mode="promise_in_bounds"
            )
    RIDX[...] = jnp.full_like(RIDX, 1024)
    for r in range(18):
        RIDX[r:r + 1, :] = recv_r[0:1, r * 128:(r + 1) * 128]
    low = lax.broadcasted_iota(jnp.int32, (128, 128), 0)
    cnum = lane.astype(f32) + 1.0
    for o in range(9):
        total = jnp.zeros((8, 128), f32)
        for h in range(2):
            ids = RIDX[2 * o + h:2 * o + h + 1, :]
            a = jnp.where(jnp.broadcast_to(ids >> 7, (8, 128)) == sub, cnum + 128.0 * h, 0.0)
            b = (jnp.broadcast_to(ids & 127, (128, 128)) == low).astype(f32)
            total = total + lax.dot_general(
                a.astype(bf16), b.astype(bf16), (((1,), (1,)), ((), ())),
                preferred_element_type=f32,
            )
        INVN[4, o] = (total + 0.5).astype(jnp.int32) - 1
    for m in range(8):
        DIAN[4, m:m + 1, :] = diag_r[0:1, m * 128:(m + 1) * 128]
    DIAN[4] = 1.0 / DIAN[4]
    for o in range(9):
        for h in range(2):
            at = jnp.broadcast_to(RIDX[2 * o + h:2 * o + h + 1, :], (8, 128))
            at = jnp.where(at == 1024, 0, at)
            cols = jnp.zeros((8, 128), f32)
            offs = jnp.zeros((8, 128), f32)
            for m in range(8):
                piece = slice(128 * m, 128 * m + 128)
                hit = (at >> 7) == m
                cols = jnp.where(hit, pick(cols_r[:, piece].astype(f32), at), cols)
                offs = jnp.where(hit, pick(off_r[:, piece], at), offs)
            MSG[o, h, 0:8, :] = cols
            MSG[o, h, 8:16, :] = offs
            MSG[o, h, 16:24, :] = at.astype(f32)
    ENT[4] = MSG[4]

    def around(src, dst, send, recv):
        out = []
        for o in AROUND:
            out.append(moved(
                (o // 3 - 1, o % 3 - 1), src(o), dst.at[8 - o], dst.at[o],
                send.at[o], recv.at[8 - o], recv.at[o],
            ))
        return out

    tables = []
    for o in AROUND:
        to = (o // 3 - 1, o % 3 - 1)
        tables.append(moved(to, INVN.at[4], INVN.at[8 - o], INVN.at[o], wsend.at[0, o], wrecv.at[0, 8 - o], wrecv.at[0, o]))
        tables.append(moved(to, DIAN.at[4], DIAN.at[8 - o], DIAN.at[o], wsend.at[1, o], wrecv.at[1, 8 - o], wrecv.at[1, o]))
    tables += around(lambda o: MSG.at[o], ENT, wsend.at[2], wrecv.at[2])

    LT[...] = jnp.zeros_like(LT)
    LT[0:32, :] = SLOT[...] & 127
    LT[...] = LT[...].T
    lane_all = lax.broadcasted_iota(jnp.int32, (128, 128), 1)
    row24 = lax.broadcasted_iota(jnp.int32, (24, 128), 0)
    for kx in range(32):
        line = jnp.broadcast_to(SLOT[kx:kx + 1, :] >> 7, (24, 128))
        HOT[:, kx * 128:(kx + 1) * 128] = (line == row24).astype(f32)
        LHOT[kx * 128:(kx + 1) * 128, :] = (
            jnp.broadcast_to(LT[:, kx:kx + 1], (128, 128)) == lane_all
        ).astype(f32).astype(bf16)
    AB[...] = jnp.zeros_like(AB)

    def edge_x(i, tiles):
        for j in tiles:
            TE[i, rows(j), :] = harmonic(PH[i, rows(j), :], PH[i + 1, rows(j), :])

    def edge_yz(i, new, done):
        for j in new:
            ctr = PH[i, rows(j), :]
            if j < TILES - 1:
                up = PH[i, 8 * j + 1:8 * j + 9, :]
            else:
                up = pltpu.roll(ctr, 7, 0)
            TN[i, rows(j), :] = harmonic(ctr, up)
            pv = PV[i, rows(j), :]
            TU[i, rows(j), :] = jnp.where(
                lane512 == NZ - 1, 0.0, harmonic(pv, pltpu.roll(pv, NZ - 1, 1))
            )
        for j in done:
            tn = TN[i, rows(j), :]
            down = TN[i, 8 * j - 1:8 * j + 7, :] if j > 0 else pltpu.roll(tn, 1, 0)
            tu = TU[i, rows(j), :]
            total = storage_coef + TE[i, rows(j), :] + TE[i - 1, rows(j), :] + tn + down + tu + pltpu.roll(tu, 1, 1)
            inv = inverse(total)
            INV[i, rows(j), :] = inv
            P1[i, rows(j), :] = (1.0 / THETA) * inv * RHS[i, rows(j), :]

    every = tuple(range(TILES))
    loop(W, W + NX - 1, lambda i: edge_x(i, (1, 2, 3, 4)))
    loop(W + 1, W + NX - 1, lambda i: edge_yz(i, (1, 2, 3), (2, 3)))

    land(first)
    go(tables)
    for near_x, next_x in ((1, 0), (NX + 2, NX + 3)):
        RKS[0, next_x] = pltpu.roll(RKS[0, near_x], 7, 0)
        RKS[1, next_x] = pltpu.roll(RKS[1, near_x], 1, 0)

    def unpack_first(i):
        got = RKS[0, i - 1]
        PH[i, rows(0), :] = jnp.where(sub512 >= 5, got, 0.0)
        PV[i, rows(0), :] = jnp.where(sub512 >= 6, pltpu.roll(got, 3, 0), 0.0)
        RHS[i, rows(0), :] = jnp.where(sub512 >= 6, pltpu.roll(got, 5, 0), 0.0)
        got = RKS[1, i - 1]
        PH[i, rows(5), :] = jnp.where(sub512 < 3, got, 0.0)
        PV[i, rows(5), :] = jnp.where(sub512 < 2, pltpu.roll(got, 5, 0), 0.0)
        RHS[i, rows(5), :] = jnp.where(sub512 < 2, pltpu.roll(got, 3, 0), 0.0)

    loop(1, NX + 5, unpack_first)
    for lo, hi in ((0, W), (W + NX - 1, 2 * W + NX - 1)):
        loop(lo, hi, lambda i: edge_x(i, every))
    loop(W, W + NX - 1, lambda i: edge_x(i, (0, 5)))
    for lo, hi in ((1, W + 1), (W + NX - 1, 2 * W + NX - 1)):
        loop(lo, hi, lambda i: edge_yz(i, every, every))
    loop(W + 1, W + NX - 1, lambda i: edge_yz(i, (0, 4, 5), (0, 1, 4, 5)))

    def residuals(field, i, tiles):
        before = None
        for j in tiles:
            ctr = field[i, rows(j), :]
            acc = RHS[i, rows(j), :] - storage_coef * ctr
            acc = acc + TE[i, rows(j), :] * (field[i + 1, rows(j), :] - ctr)
            acc = acc + TE[i - 1, rows(j), :] * (field[i - 1, rows(j), :] - ctr)
            fz = TU[i, rows(j), :] * (pltpu.roll(ctr, NZ - 1, 1) - ctr)
            acc = acc + fz - pltpu.roll(fz, 1, 1)
            up = pltpu.roll(ctr, 7, 0)
            if j < TILES - 1:
                up = jnp.where(sub512 == 7, pltpu.roll(field[i, rows(j + 1), :], 7, 0), up)
            fn = TN[i, rows(j), :] * (up - ctr)
            turned = pltpu.roll(fn, 1, 0)
            if before is not None:
                fs = jnp.where(sub512 == 0, before, turned)
            elif j > 0:
                fs = TN[i, 8 * j - 1:8 * j + 7, :] * (ctr - field[i, 8 * j - 1:8 * j + 7, :])
            else:
                fs = turned
            before = turned
            yield j, ctr, acc + fn - fs

    def sweep(extent, update):
        tiles = tuple(range(TILES)) if extent > 0 else tuple(range(1, TILES - 1))
        loop(W - extent, W + NX + extent, lambda i: update(i, tiles))

    def sweep_a(field, i, tiles):
        for j, ctr, res in residuals(field, i, tiles):
            P1[i, rows(j), :] = ctr + (1.0 / THETA) * INV[i, rows(j), :] * res

    def sweep_b_first(i, tiles):
        for j, ctr, res in residuals(P1, i, tiles):
            P0[i, rows(j), :] = (1.0 + ALPHA) * ctr + BETA * INV[i, rows(j), :] * res

    def sweep_b(old, new, i, tiles):
        for j, ctr, res in residuals(P1, i, tiles):
            new[i, rows(j), :] = (1.0 + ALPHA) * ctr - ALPHA * old[i, rows(j), :] + BETA * INV[i, rows(j), :] * res

    def exchange_pressure(field, width, slot, meanwhile=None):
        per = 8 // (2 if width == 2 else 4)
        span = 8 // per
        tiles = NX // per

        def pack(g):
            a = b = None
            for m in range(per):
                i = W + g * per + m
                one = field[i, rows(1), :]
                two = field[i, rows(4), :]
                one = one if m == 0 else pltpu.roll(one, m * span, 0)
                two = two if (m + 1) * span == 8 else pltpu.roll(two, (m + 1) * span, 0)
                a = one if a is None else jnp.where(sub512 >= m * span, one, a)
                b = two if b is None else jnp.where(sub512 >= m * span, two, b)
            PKP[0, g] = a
            PKP[1, g] = b

        loop(0, tiles, pack)
        step = []
        for dy in (-1, 1):
            side = (dy + 1) // 2
            step.append(moved(
                (0, dy), PKP.at[side, pl.ds(0, tiles)], RKP.at[slot, 1 - side, pl.ds(0, tiles)],
                RKP.at[slot, side, pl.ds(0, tiles)],
                psend.at[slot, 1, side], precv.at[slot, 1, 1 - side], precv.at[slot, 1, side],
            ))
            for dx in (-1, 1):
                far = (dx + 1) // 2
                step.append(moved(
                    (dx, dy), PKP.at[side, 0 if dx < 0 else tiles - 1], RKC.at[slot, 1 - side, 1 - far],
                    RKC.at[slot, side, far],
                    psend.at[slot, 2 + side, far], precv.at[slot, 2 + 1 - side, 1 - far], precv.at[slot, 2 + side, far],
                ))
        step += x_strips(field, field, W, width, psend.at[slot, 0], precv.at[slot, 0])
        go(step)
        if meanwhile is not None:
            meanwhile()
        land(step)

        def place(side, tile, m, i):
            if side == 0:
                turn = (8 - span - m * span) % 8
            else:
                turn = (-m * span) % 8
            tile = pltpu.roll(tile, turn, 0) if turn else tile
            field[i, rows(0 if side == 0 else 5), :] = tile

        for side, dy in ((0, -1), (1, 1)):
            _, _, there = neighbour(0, dy)

            @pl.when(there)
            def _():
                def body(g):
                    tile = RKP[slot, side, g]
                    for m in range(per):
                        place(side, tile, m, W + g * per + m)

                loop(0, tiles, body)

            for far, dx in ((0, -1), (1, 1)):
                _, _, there = neighbour(dx, dy)

                @pl.when(there)
                def _():
                    tile = RKC[slot, side, far]
                    for depth in range(width - 1):
                        if dx < 0:
                            place(side, tile, per - 1 - depth, W - 1 - depth)
                        else:
                            place(side, tile, depth, W + NX + depth)

    def restrict(field, i):
        x = i - W
        for j, _, res in residuals(field, i, tuple(range(1, TILES - 1))):
            t = j - 1
            for k in range(2):
                scaled = PR[k, x, 8 * t:8 * t + 8, :] * res
                for h in range(2):
                    both = jnp.concatenate(
                        [scaled[:, 256 * h:256 * h + 128], scaled[:, 256 * h + 128:256 * h + 256]], axis=0
                    )
                    high = both.astype(bf16)
                    at = pl.multiple_of((16 * k + x) * 128 + (t * 4 + 2 * h) * 8, 16)
                    WH[pl.ds(at, 16), :] = high
                    WL[pl.ds(at, 16), :] = (both - high.astype(f32)).astype(bf16)

    def wide(src, dst, parity, lists):
        out = []
        for n, (dx, dy) in enumerate(NEAR):
            if lists:
                def rect(ax, ay):
                    x0, x1 = max(-1, ax - 1) + 1, min(1, ax + 1) + 2
                    y0, y1 = max(-1, ay - 1) + 1, min(1, ay + 1) + 2
                    return pl.ds(x0, x1 - x0), pl.ds(y0, y1 - y0)
                give, take = rect(dx, dy), rect(-dx, -dy)
                piece, put, get = src.at[give], dst.at[(2 - dx, 2 - dy) + give], dst.at[(2 + dx, 2 + dy) + take]
            else:
                piece, put, get = src, dst.at[2 - dx, 2 - dy], dst.at[2 + dx, 2 + dy]
            outer = max(abs(dx), abs(dy)) == 2
            out.append(((10 * outer + 2 * abs(dy) + abs(dx)), moved(
                (dx, dy), piece, put, get, wsend.at[3 + parity, n], wrecv.at[3 + parity, 23 - n],
                wrecv.at[3 + parity, n],
            )))
        return [entry for _, entry in sorted(out, key=lambda pair: -pair[0])]

    def jacobi(table, near, far):
        every_row = [lambda r=r: table[r // 8, r % 8:r % 8 + 1, :] for r in range(72)]
        corner = [r for r in range(72) if r // 8 in (0, 2, 6, 8)]
        side = [r for r in range(72) if r // 8 not in (0, 2, 6, 8)]
        near()
        partly = []
        for m in range(8):
            at = cols_r[:, 128 * m:128 * m + 128]
            partly.append(pick_from(every_row, at, None, side))
        far()
        for m in range(8):
            at = cols_r[:, 128 * m:128 * m + 128]
            got = pick_from(every_row, at, partly[m], corner)
            coupled = jnp.sum(got * off_r[:, 128 * m:128 * m + 128], axis=0, keepdims=True)
            mine = table[4, m:m + 1, :]
            Y[m:m + 1, :] = mine + omega * (RATN[4, m:m + 1, :] - mine - coupled)

    def coarse(field, cycle):
        ones = jnp.ones((16, 128), bf16)
        along = (((1,), (1,)), ((), ()))
        sums = lax.dot_general(ones, WH[...], along, preferred_element_type=f32)
        sums = sums + lax.dot_general(ones, WL[...], along, preferred_element_type=f32)
        for r in range(3):
            if r < 2:
                part = HOT[8 * r:8 * r + 8, :] * sums[0:8]
            else:
                part = HOT[16:24, :] * sums[0:8]
            if r % 2 == 0:
                kept = part
            if r == 1:
                both = jnp.concatenate([kept, part], axis=0)
                high = both.astype(bf16)
                AB[0:16, :] = high
                AB[32:48, :] = (both - high.astype(f32)).astype(bf16)
            if r == 2:
                both = jnp.concatenate([part, jnp.zeros_like(part)], axis=0)
                high = both.astype(bf16)
                AB[16:32, :] = high
                AB[48:64, :] = (both - high.astype(f32)).astype(bf16)
        listed = jnp.dot(AB[...], LHOT[...], preferred_element_type=f32)
        listed = listed[0:32] + listed[32:64]
        for r in range(18):
            o, h = r // 2, r % 2
            OUT[o // 3, o % 3, h:h + 1, :] = listed[r:r + 1, :]
        step = wide(OUT, ARR, 0, True)
        go(step)
        ARR[2, 2] = OUT[...]
        if cycle == 0:
            land(tables)
        land(step)
        for p in range(9):
            total = jnp.zeros((8, 128), f32)
            for o in range(9):
                at = INVN[p, o]
                sx, sy = p // 3 + o // 3, p % 3 + o % 3
                other = 8 - o
                for h in range(2):
                    got = pick(ARR[sx, sy, other // 3, other % 3, h:h + 1, :], at)
                    total = total + jnp.where((at >> 7) == h, got, 0.0)
            ratio = total * DIAN[p]
            RATN[p] = ratio
            TAB[0, p] = omega * ratio
        jacobi(TAB.at[0], lambda: None, lambda: None)
        for s in range(1, CJ - 1):
            table = TAB.at[s % 2]
            step = around(lambda o: Y, table, csend.at[s % 2], crecv.at[s % 2])
            go(step)
            table[4] = Y[...]
            jacobi(table, lambda: land(step[4:]), lambda: land(step[:4]))
        step = wide(Y, T25, 1, False)
        go(step)
        T25[2, 2] = Y[...]
        land(step[16:])
        for o in range(9):
            BASE[o] = (1.0 - omega) * T25[1 + o // 3, 1 + o % 3] + omega * RATN[o]

        def last_rows(o, got, inside):
            ox, oy = o // 3, o % 3
            at = jnp.concatenate([ENT[o, h, 0:8, :] for h in range(2)], axis=0).astype(jnp.int32)
            chosen = [
                r for r in range(72)
                if (1 <= ox + r // 24 <= 3 and 1 <= oy + (r // 8) % 3 <= 3) == inside
            ]
            return pick_from(
                [lambda r=r: T25[ox + r // 24, oy + (r // 8) % 3, r % 8:r % 8 + 1, :] for r in range(72)],
                at, got, chosen,
            )

        for o in range(9):
            at = jnp.concatenate([ENT[o, h, 16:24, :] for h in range(2)], axis=0).astype(jnp.int32)
            LASTB[o] = pick_from([lambda r=r: BASE[o, r:r + 1, :] for r in range(8)], at)
            LASTG[o] = last_rows(o, None, True)
        land(step[:16])
        for o in range(9):
            got = LASTG[o] if o == 4 else last_rows(o, LASTG[o], False)
            for h in range(2):
                coupled = jnp.sum(got[8 * h:8 * h + 8] * ENT[o, h, 8:16, :], axis=0, keepdims=True)
                LIST[o, h:h + 1, :] = LASTB[o, 8 * h:8 * h + 1, :] - omega * coupled

        for r4 in range(4):
            VT[8 * r4:8 * r4 + 8, :] = pick_from(
                [lambda r=r: LIST[r // 2, r % 2:r % 2 + 1, :] for r in range(18)], SLOT[8 * r4:8 * r4 + 8, :]
            )
        VT[...] = VT[...].T

        def correct(x, blocks):
            for t in blocks:
                total = field[x + W, T + 8 * t:T + 8 * t + 8, :]
                for k in range(2):
                    which = jnp.full((8, 128), 16 * k, jnp.int32) + x
                    spread = []
                    for zb in range(4):
                        b0 = (t * 4 + zb) * 8
                        spread.append(
                            jnp.take_along_axis(VT[b0:b0 + 8, :], which, axis=1, mode="promise_in_bounds")
                        )
                    total = total + PR[k, x, 8 * t:8 * t + 8, :] * jnp.concatenate(spread, axis=1)
                field[x + W, T + 8 * t:T + 8 * t + 8, :] = total

        for lo in (0, NX - 2):
            correct(lo, range(4))
            correct(lo + 1, range(4))
        loop(2, NX - 2, lambda x: correct(x, (0, 3)), 4)
        return lambda: loop(2, NX - 2, lambda x: correct(x, (1, 2)), 4)

    VT[...] = jnp.zeros_like(VT)
    for cycle in range(CYCLES):
        field = (P0, P2)[cycle]
        if cycle == 0:
            sweep(1, sweep_b_first)
        else:
            exchange_pressure(field, 3, 1)
            sweep(2, functools.partial(sweep_a, field))
            sweep(1, functools.partial(sweep_b, field, field))
        loop(W, W + NX, functools.partial(restrict, field))
        rest = coarse(field, cycle)
        exchange_pressure(field, 2, 0, rest)
        sweep(1, functools.partial(sweep_a, field))
        sweep(0, functools.partial(sweep_b, field, P2))
    back = pltpu.make_async_copy(P2.at[center], out_h, in_sem.at[0])
    back.start()
    back.wait()


def shards(rhs, perm_h, perm_v, prolong, blk_slot, recv_slot, coarse_cols, coarse_off, coarse_diag):
    padded = pltpu.VMEM((2 * W + NX, 2 * T + NY, NZ), f32)
    hbm = pl.BlockSpec(memory_space=pltpu.HBM)
    i32 = jnp.int32
    return pl.pallas_call(
        kernel,
        out_shape=jax.ShapeDtypeStruct(rhs.shape, f32),
        in_specs=[hbm] * 9,
        out_specs=hbm,
        scratch_shapes=[padded] * 10
        + [
            pltpu.VMEM((2, NX, NY, NZ), f32),
            pltpu.VMEM((2, NX, 8, NZ), f32),
            pltpu.VMEM((2, 2, 8, NZ), f32),
            pltpu.VMEM((2, NX + 4, 8, NZ), f32),
            pltpu.VMEM((2, 8, 8, NZ), f32),
            pltpu.VMEM((2, 2, 8, 8, NZ), f32),
            pltpu.VMEM((2, 2, 2, 8, NZ), f32),
            pltpu.VMEM((4096, 128), bf16),
            pltpu.VMEM((4096, 128), bf16),
            pltpu.VMEM((24, 4096), f32),
            pltpu.VMEM((4096, 128), bf16),
            pltpu.VMEM((64, 4096), bf16),
            pltpu.VMEM((32, 128), i32),
            pltpu.VMEM((128, 128), i32),
            pltpu.VMEM((128, 128), f32),
            pltpu.VMEM((24, 128), i32),
            pltpu.VMEM((9, 9, 8, 128), i32),
            pltpu.VMEM((9, 8, 128), f32),
            pltpu.VMEM((9, 2, 24, 128), f32),
            pltpu.VMEM((9, 2, 24, 128), f32),
            pltpu.VMEM((3, 3, 2, 128), f32),
            pltpu.VMEM((5, 5, 3, 3, 2, 128), f32),
            pltpu.VMEM((9, 8, 128), f32),
            pltpu.VMEM((2, 9, 8, 128), f32),
            pltpu.VMEM((5, 5, 8, 128), f32),
            pltpu.VMEM((9, 2, 128), f32),
            pltpu.VMEM((8, 128), f32),
            pltpu.VMEM((9, 8, 128), f32),
            pltpu.VMEM((9, 16, 128), f32),
            pltpu.VMEM((9, 16, 128), f32),
            pltpu.VMEM((2, NX, 128), i32),
            pltpu.VMEM((1, 2304), i32),
            pltpu.VMEM((8, 1024), i32),
            pltpu.VMEM((8, 1024), f32),
            pltpu.VMEM((1, 1024), f32),
            pltpu.SemaphoreType.DMA((9,)),
            pltpu.SemaphoreType.DMA((4, 6)),
            pltpu.SemaphoreType.DMA((4, 6)),
            pltpu.SemaphoreType.DMA((2, 4, 2)),
            pltpu.SemaphoreType.DMA((2, 4, 2)),
            pltpu.SemaphoreType.DMA((2, 9)),
            pltpu.SemaphoreType.DMA((2, 9)),
            pltpu.SemaphoreType.DMA((5, 24)),
            pltpu.SemaphoreType.DMA((5, 24)),
        ],
        compiler_params=pltpu.CompilerParams(
            collective_id=0, has_side_effects=True, vmem_limit_bytes=63 << 20
        ),
    )(rhs, perm_h, perm_v, prolong, blk_slot, recv_slot.T, coarse_cols, coarse_off, coarse_diag)


def solution(mesh):
    placed = (
        P("sx", "sy", None),
        P("sx", "sy", None),
        P("sx", "sy", None),
        P(None, "sx", "sy", None),
        P(None, "sx", "sy"),
        P(None, ("sx", "sy")),
        P(None, ("sx", "sy")),
        P(None, ("sx", "sy")),
        P(None, ("sx", "sy")),
    )
    return jax.shard_map(
        shards, mesh=mesh, in_specs=placed, out_specs=P("sx", "sy", None), check_vma=False
    )
```
